128 devices in a mesh: seq: 32 (over y, x, core), ch: 4 (over z).
Axes of the slice: x: 4, y: 4, z: 4, core: 2. Of those that a mesh axis runs over, the one named last changes fastest.
Arguments:
- tokens: bfloat16 [131072, 512], P('seq', 'ch'), may hold values from -6 to 6
- norm_gain: float32 [512], P('ch'), may hold values from 0.5 to 2
- low_taps: float32 [15, 2, 512], P(None, None, 'ch'), may hold values from 0.45 to 0.75
- high_taps: float32 [15, 2, 512], P(None, None, 'ch'), may hold values from -3 to 3
- level_gain: float32 [16, 512], P(None, 'ch'), may hold values from -3 to 3
- mixing: bfloat16 [512, 512], replicated, may hold values from -0.25 to 0.25
- lengths: int32 [16], replicated, may hold values from 1 to 32768, 131072 in all
- cotangent: bfloat16 [131072, 512], P('seq', 'ch'), may hold values from -6 to 6
Outputs:
- layer_out: bfloat16 [131072, 512], P('seq', 'ch')
- grad_in: bfloat16 [131072, 512], P('seq', 'ch')
- weight_grad: float32 [512, 512], P('ch', 'seq')
The draws below stay inside these ranges and needn't reach their ends.
Inputs may be any that keep to these rules, and one draw needn't show every extreme that they name: `lengths`: the segments fill the 131072 bases exactly; the longest has exactly 32768 bases.
All inputs are finite; a program needn't handle non-finite values.
Results may differ from the reference program's by a relative error of at most 0.0035.
Values may be sent and summed in bfloat16 or wider, within the bound.
No kernel may reach another device: no remote copies, remote signals or barrier semaphores. Data moves between devices by JAX's collectives and lax.ppermute only.
A program may use at most 320 MiB of HBM per device.

```python
import math
import jax
import jax.numpy as jnp
import numpy as np
from jax import lax

C = 512
NSEG = 16
LEVELS = 15
TOKENS = 131072
SEG_MOST = 32768


def spiked(entries, own_key, source, target, shards_of, factor):
    owner, partner = [(jnp.arange(entries.shape[dim]) // (entries.shape[dim] // shards_of)).reshape([-1 if axis == dim else 1 for axis in range(entries.ndim)]) for dim in (source, target)]
    chosen = jax.random.permutation(own_key, shards_of)[partner]
    strong = (owner == chosen) | (owner == (partner + shards_of // 2) % shards_of)
    return jnp.where(strong, factor * entries, entries)


def levels(key, shape, split, least, high):
    factor_of = 1.0
    for axis_at, shards_of in split:
        heights = jax.random.uniform(jax.random.fold_in(jax.random.fold_in(key, 6), axis_at), (shards_of,), jnp.float32, least / len(split), high / len(split))
        factor_of = factor_of * jnp.repeat(jnp.exp(heights), shape[axis_at] // shards_of).reshape((-1,) + (1,) * (len(shape) - 1 - axis_at))
    return factor_of


def length_profile(count, total, limit, skew):
    weights = [(1 << 20) // math.isqrt(grade ** skew) + 1 for grade in range(2, count + 1)]
    surplus, holding = total - limit - (count - 1), [1] * (count - 1)
    while surplus > 0:
        movable = [i for i in range(count - 1) if holding[i] < limit]
        whole, left = sum([weights[i] for i in movable]), surplus
        for i in movable:
            more = min(limit - holding[i], max(1, left * weights[i] // whole), surplus)
            holding[i] = holding[i] + more
            surplus = surplus - more
    return np.array([limit] + holding)


def ragged_sizes(stream_key, number_of, total, bound, lean):
    if number_of == 2:
        one = jax.random.randint(stream_key, (), max(1, total - bound), min(bound, total - 1) + 1)
        return jnp.stack([one, total - one])
    tallies = jnp.asarray(length_profile(number_of, total, bound, lean), jnp.int32)
    twos = (number_of - 1) // 2
    donor, sink = tallies[1:1 + 2 * twos:2], tallies[2:2 + 2 * twos:2]
    margin = jnp.minimum(donor - 1, bound - sink)
    moved = jax.random.randint(jax.random.fold_in(stream_key, 1), (twos,), 0, 1 << 20) % (margin + 1)
    tallies = tallies.at[1:1 + 2 * twos:2].set(donor - moved).at[2:2 + 2 * twos:2].set(sink + moved)
    return tallies[jax.random.permutation(jax.random.fold_in(stream_key, 2), number_of)]


def noise(key, shape, deviation, limit, cuts=(), held_as=jnp.bfloat16):
    gain = levels(key, shape, cuts, -0.22, 0.18) if cuts else 1.0
    entries = jax.random.normal(key, shape, jnp.float32) * deviation * gain
    return jnp.minimum(jnp.maximum(entries, -limit), limit).astype(held_as)


def noise_with(key, dims, width, most, pieces, heavy, held_as=jnp.bfloat16):
    entries = width * jax.random.normal(key, dims, jnp.float32)
    if pieces:
        entries = entries * levels(key, dims, pieces, -0.22, 0.18)
    return jnp.clip(spiked(entries, jax.random.fold_in(key, 3), *heavy), -most, most).astype(held_as)


def setup_inputs(seed: int = 0) -> dict:
    keys = jax.random.split(jax.random.key(seed), 9)
    return {
        "tokens": noise(keys[0], (TOKENS, C), 1.0, 6.0, ((0, 32), (1, 4))),
        "norm_gain": jnp.clip(jnp.exp(math.log(2.0) - 1.3862944 * jax.random.uniform(keys[1], (C,), jnp.float32) ** levels(keys[1], (C,), ((0, 4),), -0.2, 0.2)), 0.5, 2.0),
        "low_taps": jnp.clip(0.45 + 0.3 * jax.random.uniform(keys[2], (LEVELS, 2, C), jnp.float32) ** levels(keys[2], (LEVELS, 2, C), ((2, 4),), -0.2, 0.2), 0.45, 0.75),
        "high_taps": noise(keys[3], (LEVELS, 2, C), 0.7, 3.0, ((2, 4),), jnp.float32),
        "level_gain": noise(keys[4], (LEVELS + 1, C), 0.5, 3.0, ((1, 4),), jnp.float32),
        "mixing": noise(keys[5], (C, C), C ** -0.5, 0.25),
        "lengths": ragged_sizes(keys[6], NSEG, TOKENS, SEG_MOST, 2).astype(jnp.int32),
        "cotangent": noise_with(keys[7], (TOKENS, C), 1.0, 6.0, ((0, 32), (1, 4)), (0, 1, 32, 2.75)),
    }


epsilon = 1e-06

def starts_of(positions, lengths):
    seg_ends = jnp.cumsum(lengths).astype(jnp.int32)
    before = seg_ends[None, :] <= positions[:, None]
    return lax.optimization_barrier(jnp.sum(jnp.where(before, lengths[None, :], 0), axis=1)).astype(jnp.int32)

def in_segment(positions, seg_starts, d):
    return (positions - d >= seg_starts)[:, None]

def delayed(smooth, d):
    zero_rows = jnp.zeros((d, smooth.shape[1]), smooth.dtype)
    return jnp.concatenate([zero_rows, smooth[:smooth.shape[0] - d]], axis=0)

def advanced(values, d):
    zero_rows = jnp.zeros((d, values.shape[1]), values.dtype)
    return jnp.concatenate([values[d:], zero_rows], axis=0)

def gelu_slope(pre_act):
    normal_cdf = 0.5 * (1.0 + lax.erf(pre_act * 0.7071067811865476))
    density = jnp.exp(-0.5 * pre_act * pre_act) * 0.3989422804014327
    return normal_cdf + pre_act * density

def local_forward(smooth, pre_act, positions, lengths, level_list, low_taps, high_taps, level_gain):
    seg_starts = starts_of(positions, lengths)
    for k in level_list:
        d = 2 ** k
        shifted = jnp.where(in_segment(positions, seg_starts, d), delayed(smooth, d), 0.0)
        pre_act = pre_act + level_gain[k] * (high_taps[k, 0] * smooth + high_taps[k, 1] * shifted)
        smooth = low_taps[k, 0] * smooth + low_taps[k, 1] * shifted
    return (smooth, pre_act)

def local_backward(adjoint, grad_pre, positions, lengths, level_list, low_taps, high_taps, level_gain):
    seg_starts = starts_of(positions, lengths)
    for k in level_list:
        d = 2 ** k
        grad_high = level_gain[k] * grad_pre
        passed = jnp.where(in_segment(positions, seg_starts, d), high_taps[k, 1] * grad_high + low_taps[k, 1] * adjoint, 0.0)
        adjoint = low_taps[k, 0] * adjoint + high_taps[k, 0] * grad_high + advanced(passed, d)
    return adjoint

def reference(tokens, norm_gain, low_taps, high_taps, level_gain, mixing, lengths, cotangent):
    inputs = tokens.astype(jnp.float32)
    positions = jnp.arange(inputs.shape[0], dtype=jnp.int32)
    inv_rms = lax.rsqrt(lax.optimization_barrier(jnp.mean(inputs * inputs, axis=1, keepdims=True)) + epsilon)
    normed = inputs * inv_rms * norm_gain
    smooth, pre_act = local_forward(normed, jnp.zeros_like(normed), positions, lengths, list(range(LEVELS)), low_taps, high_taps, level_gain)
    pre_act = pre_act + level_gain[LEVELS] * smooth
    hidden = jax.nn.gelu(pre_act, approximate=False).astype(jnp.bfloat16)
    layer_out = (inputs + jnp.dot(hidden, mixing, preferred_element_type=jnp.float32)).astype(jnp.bfloat16)
    weight_grad = jnp.dot(hidden.T, cotangent, preferred_element_type=jnp.float32) / math.sqrt(TOKENS)
    grad_hidden = jnp.dot(cotangent, mixing.T, preferred_element_type=jnp.float32)
    grad_pre = grad_hidden * gelu_slope(pre_act)
    adjoint = local_backward(level_gain[LEVELS] * grad_pre, grad_pre, positions, lengths, list(reversed(range(LEVELS))), low_taps, high_taps, level_gain)
    inner_sum = lax.optimization_barrier(jnp.mean(norm_gain * adjoint * inputs, axis=1, keepdims=True))
    grad_in = cotangent.astype(jnp.float32) + inv_rms * norm_gain * adjoint - inputs * inv_rms ** 3 * inner_sum
    return (layer_out, grad_in.astype(jnp.bfloat16), weight_grad)
```

```python
import math

import jax
import jax.numpy as jnp
from jax import lax
from jax.experimental import pallas as pl
from jax.experimental.pallas import tpu as pltpu
from jax.sharding import PartitionSpec as P

LEVELS = 15
LANES = 128
NCH = 4
SEQ = 32
ZN = 4
ROWS = 1024
LOCAL = 32
PAD = 128
BLK = 32
EPS = 1e-06
F32 = jnp.float32
BF16 = jnp.bfloat16
VMEM = pltpu.VMEM
SMEM = pltpu.SMEM


def params():
    return pltpu.CompilerParams(vmem_limit_bytes=48 * 1024 * 1024)


def vspec():
    return pl.BlockSpec(memory_space=VMEM)


def sspec():
    return pl.BlockSpec(memory_space=SMEM)


def cost(flops, nbytes):
    return pl.CostEstimate(flops=flops, bytes_accessed=nbytes, transcendentals=0)


def turn_kernel(x_ref, xt_ref, ss_ref, scr):
    def one(m, _):
        r = pl.multiple_of(m * LANES, LANES)
        t = x_ref[pl.ds(r, LANES), :].astype(F32).T
        scr[pl.ds(r, LANES), :] = t
        ss_ref[pl.ds(m, 1), :] = jnp.sum(t * t, axis=0, keepdims=True)
        return 0

    lax.fori_loop(0, LOCAL, one, 0)

    def two(g, _):
        for i in range(NCH):
            xt_ref[g, i] = scr[pl.ds(i * SEQ + g, LOCAL, stride=LANES), :].astype(BF16)
        return 0

    lax.fori_loop(0, SEQ, two, 0)


def turn(x):
    return pl.pallas_call(
        turn_kernel,
        out_shape=(
            jax.ShapeDtypeStruct((SEQ, NCH, LOCAL, LANES), BF16),
            jax.ShapeDtypeStruct((LOCAL, LANES), F32),
        ),
        in_specs=[vspec()],
        out_specs=(vspec(), vspec()),
        scratch_shapes=[VMEM((LOCAL * LANES, LANES), F32)],
        compiler_params=params(),
        cost_estimate=cost(10**6, 3 * 10**6),
        name="turn",
    )(x)


def rel_kernel(len_ref, rel_ref):
    starts = []
    at = jnp.int32(0)
    for n in range(16):
        at = at + len_ref[n]
        starts.append(at)

    def one(b, _):
        r = pl.multiple_of(b * BLK, BLK)
        row = lax.broadcasted_iota(jnp.int32, (BLK, LANES), 0) + r
        t = row * LANES + lax.broadcasted_iota(jnp.int32, (BLK, LANES), 1)
        start = jnp.zeros((BLK, LANES), jnp.int32)
        for n in range(15):
            start = jnp.where(t >= starts[n], starts[n], start)
        rel_ref[pl.ds(r, BLK), :] = jnp.where(row < ROWS, t - start, -1)
        return 0

    lax.fori_loop(0, (ROWS + PAD + BLK) // BLK, one, 0)


def rel_of(lengths):
    return pl.pallas_call(
        rel_kernel,
        out_shape=jax.ShapeDtypeStruct((ROWS + PAD + BLK, LANES), jnp.int32),
        in_specs=[sspec()],
        out_specs=vspec(),
        compiler_params=params(),
        cost_estimate=cost(10**7, 10**6),
        name="rel",
    )(lengths)


def grad_hidden_kernel(cot_ref, mix_ref, out_ref, scr):
    def one(m, _):
        r = pl.multiple_of(m * LANES, LANES)
        acc = None
        for c in range(ZN):
            part = lax.dot_general(
                mix_ref[:, c * LANES : (c + 1) * LANES],
                cot_ref[c, pl.ds(r, LANES), :],
                (((1,), (1,)), ((), ())),
                preferred_element_type=F32,
            )
            acc = part if acc is None else acc + part
        scr[pl.ds(pl.multiple_of(m * 512, 512), 512), :] = acc
        return 0

    lax.fori_loop(0, 8, one, 0)

    def two(g, _):
        for c in range(ZN):
            rows = [
                scr[pl.ds(c * LANES + i * SEQ + g, 8, stride=512), :] for i in range(NCH)
            ]
            out_ref[g * ZN + c] = jnp.concatenate(rows, axis=0).astype(BF16)
        return 0

    lax.fori_loop(0, SEQ, two, 0)


def grad_hidden_of(cot_rows, mixing):
    return pl.pallas_call(
        grad_hidden_kernel,
        out_shape=jax.ShapeDtypeStruct((SEQ * ZN, 32, LANES), BF16),
        in_specs=[vspec(), vspec()],
        out_specs=vspec(),
        scratch_shapes=[VMEM((8 * 512, LANES), F32)],
        compiler_params=params(),
        cost_estimate=cost(5 * 10**8, 3 * 10**6),
        name="grad_hidden",
    )(cot_rows, mixing)


def forward_kernel(x_ref, inv_ref, rel_ref, c_ref, w_ref, gain_ref, hid_ref, slope_ref, z, y):
    lane = lax.broadcasted_iota(jnp.int32, (BLK, LANES), 1)
    for i in range(NCH):
        z[i, pl.ds(0, PAD), :] = jnp.zeros((PAD, LANES), F32)

    def load(s, _):
        r = pl.multiple_of(s * LOCAL, LOCAL)
        inv = inv_ref[s]
        for i in range(NCH):
            z[i, pl.ds(PAD + r, LOCAL), :] = x_ref[s, i].astype(F32) * inv * gain_ref[i]
        return 0

    lax.fori_loop(0, SEQ, load, 0)

    for k in range(LEVELS):
        d = 2**k

        def level(b, _, k=k, d=d):
            r = pl.multiple_of(ROWS - BLK - b * BLK, BLK)
            inside = rel_ref[pl.ds(r, BLK), :] >= d
            for i in range(NCH):
                here = z[i, pl.ds(PAD + r, BLK), :]
                if d < LANES:
                    back = z[i, pl.ds(PAD + r - 1, BLK), :]
                    back = pltpu.roll(jnp.where(lane >= LANES - d, back, here), d, 1)
                else:
                    back = z[i, pl.ds(PAD + r - d // LANES, BLK), :]
                back = jnp.where(inside, back, 0.0)
                part = w_ref[k * NCH + i] * here
                if k > 0:
                    part = y[i, pl.ds(r, BLK), :] + part
                new = here + c_ref[k * NCH + i] * back
                if k == LEVELS - 1:
                    part = part + w_ref[LEVELS * NCH + i] * new
                else:
                    z[i, pl.ds(PAD + r, BLK), :] = new
                y[i, pl.ds(r, BLK), :] = part
            return 0

        lax.fori_loop(0, ROWS // BLK, level, 0)

    def finish(j, _):
        r = pl.multiple_of(j * 8, 8)
        rows = []
        for i in range(NCH):
            v = y[i, pl.ds(r, 8), :]
            cdf = 0.5 * (1.0 + lax.erf(v * 0.7071067811865476))
            density = jnp.exp(-0.5 * v * v) * 0.3989422804014327
            rows.append(v * cdf)
            slope_ref[i, pl.ds(r, 8), :] = cdf + v * density
        hid_ref[j] = jnp.concatenate(rows, axis=0).astype(BF16)
        return 0

    lax.fori_loop(0, ROWS // 8, finish, 0)


def forward(x, inv, rel, coef, weight, gain):
    return pl.pallas_call(
        forward_kernel,
        out_shape=(
            jax.ShapeDtypeStruct((SEQ * ZN, 32, LANES), BF16),
            jax.ShapeDtypeStruct((NCH, ROWS, LANES), F32),
        ),
        in_specs=[vspec(), vspec(), vspec(), sspec(), sspec(), sspec()],
        out_specs=(vspec(), vspec()),
        scratch_shapes=[
            VMEM((NCH, PAD + ROWS, LANES), F32),
            VMEM((NCH, ROWS, LANES), F32),
        ],
        compiler_params=params(),
        cost_estimate=cost(10**8, 6 * 10**6),
        name="forward",
    )(x, inv, rel, coef, weight, gain)


def backward_kernel(gh_ref, slope_ref, rel_ref, c_ref, w_ref, out_ref, grad, v):
    lane = lax.broadcasted_iota(jnp.int32, (BLK, LANES), 1)

    def load(j, _):
        r = pl.multiple_of(j * 8, 8)
        block = gh_ref[j].astype(F32)
        for i in range(NCH):
            g = block[i * 8 : (i + 1) * 8] * slope_ref[i, pl.ds(r, 8), :]
            grad[i, pl.ds(r, 8), :] = g
            v[i, pl.ds(r, 8), :] = w_ref[LEVELS * NCH + i] * g
        return 0

    lax.fori_loop(0, ROWS // 8, load, 0)
    for i in range(NCH):
        v[i, pl.ds(ROWS, PAD), :] = jnp.zeros((PAD, LANES), F32)

    for k in range(LEVELS - 1, -1, -1):
        d = 2**k

        def level(b, _, k=k, d=d):
            r = pl.multiple_of(b * BLK, BLK)
            if d < LANES:
                low = lane < d
                rel = jnp.where(low, rel_ref[pl.ds(r + 1, BLK), :], rel_ref[pl.ds(r, BLK), :])
            else:
                rel = rel_ref[pl.ds(r + d // LANES, BLK), :]
            inside = rel >= d
            for i in range(NCH):
                here = v[i, pl.ds(r, BLK), :]
                if d < LANES:
                    ahead = jnp.where(low, v[i, pl.ds(r + 1, BLK), :], here)
                    ahead = pltpu.roll(jnp.where(inside, ahead, 0.0), LANES - d, 1)
                else:
                    ahead = jnp.where(inside, v[i, pl.ds(r + d // LANES, BLK), :], 0.0)
                g = grad[i, pl.ds(r, BLK), :]
                new = here + w_ref[k * NCH + i] * g + c_ref[k * NCH + i] * ahead
                if k == 0:
                    out_ref[b, i] = new.astype(BF16)
                else:
                    v[i, pl.ds(r, BLK), :] = new
            return 0

        lax.fori_loop(0, ROWS // BLK, level, 0)


def backward(gh, slope, rel, coef, weight):
    return pl.pallas_call(
        backward_kernel,
        out_shape=jax.ShapeDtypeStruct((SEQ, NCH, LOCAL, LANES), BF16),
        in_specs=[vspec(), vspec(), vspec(), sspec(), sspec()],
        out_specs=vspec(),
        scratch_shapes=[
            VMEM((NCH, ROWS, LANES), F32),
            VMEM((NCH, ROWS + PAD, LANES), F32),
        ],
        compiler_params=params(),
        cost_estimate=cost(10**8, 6 * 10**6),
        name="backward",
    )(gh, slope, rel, coef, weight)


def mix_kernel(hid_ref, cot_ref, x_ref, mix_ref, out_ref, wg_ref, scr, acc):
    def load(j, _):
        scr[pl.ds(pl.multiple_of(j * 32, 32), 32), :] = hid_ref[j].astype(F32)
        return 0

    lax.fori_loop(0, SEQ * ZN, load, 0)
    acc[...] = jnp.zeros_like(acc)

    def one(m, _):
        r = pl.multiple_of(m * LANES, LANES)
        rows = [
            scr[pl.ds(c * 32 + i * 8 + m, SEQ, stride=LANES), :]
            for c in range(ZN)
            for i in range(NCH)
        ]
        h = jnp.concatenate(rows, axis=0)
        hb = h.astype(BF16)
        ht = h.T.astype(BF16)
        mixed = jnp.dot(ht, mix_ref[...], preferred_element_type=F32)
        for c in range(ZN):
            out_ref[c, pl.ds(r, LANES), :] = (
                x_ref[c, pl.ds(r, LANES), :].astype(F32) + mixed[:, c * LANES : (c + 1) * LANES]
            ).astype(BF16)
            acc[c] += jnp.dot(hb, cot_ref[c, pl.ds(r, LANES), :], preferred_element_type=F32)
        return 0

    lax.fori_loop(0, 8, one, 0)
    for j in range(ZN):
        for c in range(ZN):
            t = acc[j, pl.ds(c * LANES, LANES), :].T
            for s in range(8):
                wg_ref[(j * 8 + s) * ZN + c] = t[s * 16 : (s + 1) * 16]


def mix(hid, cot_rows, x_rows, mixing):
    return pl.pallas_call(
        mix_kernel,
        out_shape=(
            jax.ShapeDtypeStruct((ZN, ROWS, LANES), BF16),
            jax.ShapeDtypeStruct((SEQ * ZN, 16, LANES), F32),
        ),
        in_specs=[vspec()] * 4,
        out_specs=(vspec(), vspec()),
        scratch_shapes=[
            VMEM((SEQ * ZN * 32, LANES), F32),
            VMEM((ZN, 512, LANES), F32),
        ],
        compiler_params=params(),
        cost_estimate=cost(10**9, 6 * 10**6),
        name="mix",
    )(hid, cot_rows, x_rows, mixing)


def inner_kernel(v_ref, xt_ref, gain_ref, out_ref):
    def one(g, acc):
        for i in range(NCH):
            acc = acc + gain_ref[i * SEQ + g] * (v_ref[g, i].astype(F32) * xt_ref[g, i].astype(F32))
        return acc

    out_ref[...] = lax.fori_loop(0, SEQ, one, jnp.zeros((LOCAL, LANES), F32))


def inner(v, xt, gain):
    return pl.pallas_call(
        inner_kernel,
        out_shape=jax.ShapeDtypeStruct((LOCAL, LANES), F32),
        in_specs=[vspec(), vspec(), sspec()],
        out_specs=vspec(),
        compiler_params=params(),
        cost_estimate=cost(10**6, 2 * 10**6),
        name="inner",
    )(v, xt, gain)


def grad_in_kernel(v_ref, xt_ref, cot_ref, inv_ref, mean_ref, gain_ref, out_ref, scr):
    inv = inv_ref[...]
    scale = inv * inv * inv * mean_ref[...]

    def one(g, _):
        for i in range(NCH):
            c = i * SEQ + g
            u = gain_ref[c] * inv * v_ref[g, i].astype(F32) - scale * xt_ref[g, i].astype(F32)
            scr[pl.ds(pl.multiple_of(c * LOCAL, LOCAL), LOCAL), :] = u
        return 0

    lax.fori_loop(0, SEQ, one, 0)

    def two(m, _):
        r = pl.multiple_of(m * LANES, LANES)
        u = scr[pl.ds(m, LANES, stride=LOCAL), :].T
        out_ref[pl.ds(r, LANES), :] = (cot_ref[pl.ds(r, LANES), :].astype(F32) + u).astype(BF16)
        return 0

    lax.fori_loop(0, LOCAL, two, 0)


def grad_in_of(v, xt, cot, inv, mean, gain):
    return pl.pallas_call(
        grad_in_kernel,
        out_shape=jax.ShapeDtypeStruct((LOCAL * LANES, LANES), BF16),
        in_specs=[vspec()] * 5 + [sspec()],
        out_specs=vspec(),
        scratch_shapes=[VMEM((LOCAL * LANES, LANES), F32)],
        compiler_params=params(),
        cost_estimate=cost(10**7, 5 * 10**6),
        name="grad_in",
    )(v, xt, cot, inv, mean, gain)


def exchange(a, axes):
    return lax.all_to_all(a, axes, 0, 0, tiled=True)


def sum_over_ch(a):
    total = a
    for by in (1, 2, 3):
        total = total + lax.ppermute(a, "ch", [(j, (j + by) % ZN) for j in range(ZN)])
    return total


def own_channels(a, g):
    return lax.dynamic_index_in_dim(a.reshape(a.shape[:-1] + (NCH, SEQ)), g, a.ndim, False)


def level_weights(low, high, gain):
    low0, low1 = low[:, 0], low[:, 1]
    high0, high1 = high[:, 0], high[:, 1]
    ratio = gain[:LEVELS] * high1 / low1
    zero = jnp.zeros_like(ratio[:1])
    weight = jnp.concatenate([gain[:LEVELS] * high0 - ratio * low0, gain[LEVELS:]], axis=0)
    weight = weight + jnp.concatenate([zero, ratio], axis=0)
    scale = [jnp.ones_like(low0[0])]
    for k in range(LEVELS):
        scale.append(scale[-1] * low0[k])
    return (low1 / low0).reshape(-1), (weight * jnp.stack(scale)).reshape(-1)


def per_device(tokens, norm_gain, low_taps, high_taps, level_gain, mixing, lengths, cotangent):
    both = ("seq", "ch")
    g = lax.axis_index("seq")
    full = mixing.shape[0]
    bases = LOCAL * LANES * SEQ

    xt, squares = turn(tokens)
    x_seq = exchange(xt, "seq")
    cot_rows = exchange(cotangent.reshape(ZN, ROWS, LANES), "ch")
    x_rows = exchange(tokens.reshape(ZN, ROWS, LANES), "ch")
    inv = lax.rsqrt(sum_over_ch(squares) / full + EPS)
    inv_seq = exchange(jnp.broadcast_to(inv[None], (SEQ, LOCAL, LANES)), "seq")
    rel = rel_of(lengths)
    coef, weight = level_weights(
        own_channels(low_taps, g), own_channels(high_taps, g), own_channels(level_gain, g)
    )
    gh_seq = exchange(grad_hidden_of(cot_rows, mixing), both)
    hid, slope = forward(x_seq, inv_seq, rel, coef, weight, own_channels(norm_gain, g))
    hid_rows = exchange(hid, both)
    v = exchange(backward(gh_seq, slope, rel, coef, weight), "seq")
    out_rows, wg = mix(hid_rows, cot_rows, x_rows, mixing)
    layer_out = exchange(out_rows, "ch").reshape(LOCAL * LANES, LANES)
    weight_grad = jnp.sum(exchange(wg, both), axis=0).T / math.sqrt(bases)
    mean = sum_over_ch(inner(v, xt, norm_gain)) / full
    grad_in = grad_in_of(v, xt, cotangent, inv, mean, norm_gain)
    return (layer_out, grad_in, weight_grad)


def solution(mesh):
    in_specs = (
        P("seq", "ch"),
        P("ch"),
        P(None, None, "ch"),
        P(None, None, "ch"),
        P(None, "ch"),
        P(),
        P(),
        P("seq", "ch"),
    )
    out_specs = (P("seq", "ch"), P("seq", "ch"), P("ch", "seq"))
    return jax.shard_map(
        per_device, mesh=mesh, in_specs=in_specs, out_specs=out_specs, check_vma=False
    )
```

```python
import functools
import math

import jax
import jax.numpy as jnp
from jax import lax
from jax.experimental import pallas as pl
from jax.experimental.pallas import tpu as pltpu
from jax.sharding import PartitionSpec as P

LEVELS = 15
LANES = 128
NCH = 4
SEQ = 32
ZN = 4
ROWS = 1024
LOCAL = 32
FWD = 4
BWD = 4
EPS = 1e-06
F32 = jnp.float32
BF16 = jnp.bfloat16
VMEM = pltpu.VMEM
SMEM = pltpu.SMEM


def params():
    return pltpu.CompilerParams(vmem_limit_bytes=48 * 1024 * 1024)


def vspec():
    return pl.BlockSpec(memory_space=VMEM)


def sspec():
    return pl.BlockSpec(memory_space=SMEM)


def cost(flops, nbytes):
    return pl.CostEstimate(flops=flops, bytes_accessed=nbytes, transcendentals=0)


def turn_kernel(x_ref, xt_ref, ss_ref, scr):
    def one(m, _):
        r = pl.multiple_of(m * LANES, LANES)
        t = x_ref[pl.ds(r, LANES), :].astype(F32).T
        j = (m % 4) * 8 + m // 4
        scr[pl.ds(pl.multiple_of(j * LANES, LANES), LANES), :] = t
        ss_ref[pl.ds(j, 1), :] = jnp.sum(t * t, axis=0, keepdims=True)
        return 0

    lax.fori_loop(0, LOCAL, one, 0)

    def two(g, _):
        for i in range(NCH):
            xt_ref[g, i] = scr[pl.ds(i * SEQ + g, LOCAL, stride=LANES), :].astype(BF16)
        return 0

    lax.fori_loop(0, SEQ, two, 0)


def turn(x):
    return pl.pallas_call(
        turn_kernel,
        out_shape=(
            jax.ShapeDtypeStruct((SEQ, NCH, LOCAL, LANES), BF16),
            jax.ShapeDtypeStruct((LOCAL, LANES), F32),
        ),
        in_specs=[vspec()],
        out_specs=(vspec(), vspec()),
        scratch_shapes=[VMEM((LOCAL * LANES, LANES), F32)],
        compiler_params=params(),
        cost_estimate=cost(10**6, 3 * 10**6),
        name="turn",
    )(x)


def rel_kernel(len_ref, rel_ref):
    starts = []
    at = jnp.int32(0)
    for n in range(15):
        at = at + len_ref[n]
        starts.append(at)
    shape = (4, 8, LANES)
    base = (
        lax.broadcasted_iota(jnp.int32, shape, 0) * LANES
        + lax.broadcasted_iota(jnp.int32, shape, 1) * 512
        + lax.broadcasted_iota(jnp.int32, shape, 2)
    )

    def one(s, _):
        t = base + s * (LOCAL * LANES)
        start = jnp.zeros(shape, jnp.int32)
        for n in range(15):
            start = jnp.where(t >= starts[n], starts[n], start)
        rel_ref[s] = t - start
        return 0

    lax.fori_loop(0, SEQ, one, 0)


def rel_of(lengths):
    return pl.pallas_call(
        rel_kernel,
        out_shape=jax.ShapeDtypeStruct((SEQ, 4, 8, LANES), jnp.int32),
        in_specs=[sspec()],
        out_specs=vspec(),
        compiler_params=params(),
        cost_estimate=cost(10**7, 10**6),
        name="rel",
    )(lengths)


def grad_hidden_kernel(cot_ref, mix_ref, out_ref, scr):
    def one(m, _):
        r = pl.multiple_of(m * LANES, LANES)
        acc = None
        for c in range(ZN):
            part = lax.dot_general(
                mix_ref[:, c * LANES : (c + 1) * LANES],
                cot_ref[c, pl.ds(r, LANES), :],
                (((1,), (1,)), ((), ())),
                preferred_element_type=F32,
            )
            acc = part if acc is None else acc + part
        scr[pl.ds(pl.multiple_of(m * 512, 512), 512), :] = acc
        return 0

    lax.fori_loop(0, 8, one, 0)

    def two(g, _):
        for c in range(ZN):
            rows = [
                scr[pl.ds(c * LANES + i * SEQ + g, 8, stride=512), :] for i in range(NCH)
            ]
            out_ref[g * ZN + c] = jnp.concatenate(rows, axis=0).astype(BF16)
        return 0

    lax.fori_loop(0, SEQ, two, 0)


def grad_hidden_of(cot_rows, mixing):
    return pl.pallas_call(
        grad_hidden_kernel,
        out_shape=jax.ShapeDtypeStruct((SEQ * ZN, 32, LANES), BF16),
        in_specs=[vspec(), vspec()],
        out_specs=vspec(),
        scratch_shapes=[VMEM((8 * 512, LANES), F32)],
        compiler_params=params(),
        cost_estimate=cost(5 * 10**8, 3 * 10**6),
        name="grad_hidden",
    )(cot_rows, mixing)


def forward_kernel(FWD, x_ref, inv_ref, rel_ref, c_ref, w_ref, gain_ref, hid_ref, slope_ref, near, far):
    near[...] = jnp.zeros_like(near)
    far[...] = jnp.zeros_like(far)
    lane = lax.broadcasted_iota(jnp.int32, (8, LANES), 1)
    sub = lax.broadcasted_iota(jnp.int32, (8, LANES), 0)

    def before(now, old, by):
        return jnp.concatenate([old, now], axis=0)[old.shape[0] - by :][: now.shape[0]]

    def step(b, _):
        s = b * FWD
        rel = rel_ref[pl.ds(s, FWD)]
        inside = [rel >= 2**k for k in range(LEVELS)]
        inv = inv_ref[pl.ds(s, FWD)]
        for pair in range(0, NCH, 2):
            hidden = []
            for i in (pair, pair + 1):
                z = x_ref[pl.ds(s, FWD), i].astype(F32) * (inv * gain_ref[i])
                z = z.reshape(FWD, 4, 8, LANES)
                y = w_ref[i] * z
                for k in range(LEVELS):
                    d = 2**k
                    if k < 8:
                        last = z[:, 3]
                        prev = before(last, near[k, i, pl.ds(3, 1)], 1)
                        near[k, i, pl.ds(3, 1)] = last[FWD - 1 :]
                        first = pltpu.roll(jnp.where(sub == 7, prev, last), 1, 1)
                        back = jnp.concatenate([first[:, None], z[:, :3]], axis=1)
                        if d < LANES:
                            back = pltpu.roll(jnp.where(lane >= LANES - d, back, z), d, 3)
                    elif k == 8:
                        last = z[:, 2:]
                        prev = before(last, near[k, i, pl.ds(2, 2)][None], 1)
                        near[k, i, pl.ds(2, 2)] = last[FWD - 1]
                        first = pltpu.roll(jnp.where(sub == 7, prev, last), 1, 2)
                        back = jnp.concatenate([first, z[:, :2]], axis=1)
                    elif k < 12:
                        by = 2 ** (k - 9)
                        prev = before(z, near[k, i][None], 1)
                        near[k, i] = z[FWD - 1]
                        back = pltpu.roll(jnp.where(sub >= 8 - by, prev, z), by, 2)
                    else:
                        by = 2 ** (k - 12)
                        old = far[k - 12, i]
                        back = before(z, old, by)
                        far[k - 12, i] = jnp.concatenate([old, z], axis=0)[FWD:]
                    z = z + c_ref[k * NCH + i] * jnp.where(inside[k], back, 0.0)
                    y = y + w_ref[(k + 1) * NCH + i] * z
                cdf = 0.5 * (1.0 + lax.erf(y * 0.7071067811865476))
                density = jnp.exp(-0.5 * y * y) * 0.3989422804014327
                slope_ref[i, pl.ds(s, FWD)] = cdf + y * density
                hidden.append(y * cdf)
            hid_ref[pl.ds(s, FWD), :, pl.ds(pair * 8, 16), :] = jnp.concatenate(
                hidden, axis=2
            ).astype(BF16)
        return 0

    lax.fori_loop(0, SEQ // FWD, step, 0)


def forward(x, inv, rel, coef, weight, gain):
    return pl.pallas_call(
        functools.partial(forward_kernel, FWD),
        out_shape=(
            jax.ShapeDtypeStruct((SEQ, ZN, 32, LANES), BF16),
            jax.ShapeDtypeStruct((NCH, SEQ, 4, 8, LANES), F32),
        ),
        in_specs=[vspec(), vspec(), vspec(), sspec(), sspec(), sspec()],
        out_specs=(vspec(), vspec()),
        scratch_shapes=[
            VMEM((12, NCH, 4, 8, LANES), F32),
            VMEM((3, NCH, 4, 4, 8, LANES), F32),
        ],
        compiler_params=params(),
        cost_estimate=cost(10**8, 6 * 10**6),
        name="forward",
    )(x, inv, rel, coef, weight, gain)


def backward_kernel(BWD, gh_ref, slope_ref, rel_ref, c_ref, w_ref, out_ref, near, far):
    near[...] = jnp.zeros_like(near)
    far[...] = jnp.zeros_like(far)
    lane = lax.broadcasted_iota(jnp.int32, (8, LANES), 1)
    sub = lax.broadcasted_iota(jnp.int32, (8, LANES), 0)

    def after(now, old, by):
        return jnp.concatenate([now, old], axis=0)[by:][: now.shape[0]]

    def step(b, _):
        s = SEQ - BWD - b * BWD
        rel = rel_ref[pl.ds(s, BWD)]
        inside = [rel >= 2**k for k in range(LEVELS)]
        for pair in range(0, NCH, 2):
            block = gh_ref[pl.ds(s, BWD), :, pl.ds(pair * 8, 16), :].astype(F32)
            for i in (pair, pair + 1):
                grad = block[:, :, (i - pair) * 8 : (i - pair + 1) * 8]
                grad = grad * slope_ref[i, pl.ds(s, BWD)]
                v = w_ref[LEVELS * NCH + i] * grad
                for k in range(LEVELS - 1, -1, -1):
                    d = 2**k
                    p = jnp.where(inside[k], v, 0.0)
                    if k < 8:
                        head = p[:, 0]
                        foll = after(head, near[k, i, pl.ds(0, 1)], 1)
                        near[k, i, pl.ds(0, 1)] = head[:1]
                        end = pltpu.roll(jnp.where(sub == 0, foll, head), 7, 1)
                        ahead = jnp.concatenate([p[:, 1:], end[:, None]], axis=1)
                        if d < LANES:
                            ahead = pltpu.roll(jnp.where(lane < d, ahead, p), LANES - d, 3)
                    elif k == 8:
                        head = p[:, :2]
                        foll = after(head, near[k, i, pl.ds(0, 2)][None], 1)
                        near[k, i, pl.ds(0, 2)] = head[0]
                        end = pltpu.roll(jnp.where(sub == 0, foll, head), 7, 2)
                        ahead = jnp.concatenate([p[:, 2:], end], axis=1)
                    elif k < 12:
                        by = 2 ** (k - 9)
                        foll = after(p, near[k, i][None], 1)
                        near[k, i] = p[0]
                        ahead = pltpu.roll(jnp.where(sub < by, foll, p), 8 - by, 2)
                    else:
                        by = 2 ** (k - 12)
                        old = far[k - 12, i]
                        ahead = after(p, old, by)
                        far[k - 12, i] = jnp.concatenate([p, old], axis=0)[:4]
                    v = v + w_ref[k * NCH + i] * grad + c_ref[k * NCH + i] * ahead
                out_ref[pl.ds(s, BWD), i] = v.reshape(BWD, 32, LANES).astype(BF16)
        return 0

    lax.fori_loop(0, SEQ // BWD, step, 0)


def backward(gh, slope, rel, coef, weight):
    return pl.pallas_call(
        functools.partial(backward_kernel, BWD),
        out_shape=jax.ShapeDtypeStruct((SEQ, NCH, LOCAL, LANES), BF16),
        in_specs=[vspec(), vspec(), vspec(), sspec(), sspec()],
        out_specs=vspec(),
        scratch_shapes=[
            VMEM((12, NCH, 4, 8, LANES), F32),
            VMEM((3, NCH, 4, 4, 8, LANES), F32),
        ],
        compiler_params=params(),
        cost_estimate=cost(10**8, 6 * 10**6),
        name="backward",
    )(gh, slope, rel, coef, weight)


def mix_kernel(hid_ref, cot_ref, x_ref, mix_ref, out_ref, wg_ref, scr, acc):
    def load(j, _):
        scr[pl.ds(pl.multiple_of(j * 32, 32), 32), :] = hid_ref[j].astype(F32)
        return 0

    lax.fori_loop(0, SEQ * ZN, load, 0)
    acc[...] = jnp.zeros_like(acc)

    def one(m, _):
        r = pl.multiple_of(m * LANES, LANES)
        rows = [
            scr[pl.ds(c * 32 + i * 8 + m, SEQ, stride=LANES), :]
            for c in range(ZN)
            for i in range(NCH)
        ]
        h = jnp.concatenate(rows, axis=0)
        hb = h.astype(BF16)
        ht = h.T.astype(BF16)
        mixed = jnp.dot(ht, mix_ref[...], preferred_element_type=F32)
        for c in range(ZN):
            out_ref[c, pl.ds(r, LANES), :] = (
                x_ref[c, pl.ds(r, LANES), :].astype(F32) + mixed[:, c * LANES : (c + 1) * LANES]
            ).astype(BF16)
            acc[c] += jnp.dot(hb, cot_ref[c, pl.ds(r, LANES), :], preferred_element_type=F32)
        return 0

    lax.fori_loop(0, 8, one, 0)
    for j in range(ZN):
        for c in range(ZN):
            t = acc[j, pl.ds(c * LANES, LANES), :].T
            for s in range(8):
                wg_ref[(j * 8 + s) * ZN + c] = t[s * 16 : (s + 1) * 16]


def mix(hid, cot_rows, x_rows, mixing):
    return pl.pallas_call(
        mix_kernel,
        out_shape=(
            jax.ShapeDtypeStruct((ZN, ROWS, LANES), BF16),
            jax.ShapeDtypeStruct((SEQ * ZN, 16, LANES), F32),
        ),
        in_specs=[vspec()] * 4,
        out_specs=(vspec(), vspec()),
        scratch_shapes=[
            VMEM((SEQ * ZN * 32, LANES), F32),
            VMEM((ZN, 512, LANES), F32),
        ],
        compiler_params=params(),
        cost_estimate=cost(10**9, 6 * 10**6),
        name="mix",
    )(hid, cot_rows, x_rows, mixing)


def inner_kernel(v_ref, xt_ref, gain_ref, out_ref):
    def one(g, acc):
        for i in range(NCH):
            acc = acc + gain_ref[i * SEQ + g] * (v_ref[g, i].astype(F32) * xt_ref[g, i].astype(F32))
        return acc

    out_ref[...] = lax.fori_loop(0, SEQ, one, jnp.zeros((LOCAL, LANES), F32))


def inner(v, xt, gain):
    return pl.pallas_call(
        inner_kernel,
        out_shape=jax.ShapeDtypeStruct((LOCAL, LANES), F32),
        in_specs=[vspec(), vspec(), sspec()],
        out_specs=vspec(),
        compiler_params=params(),
        cost_estimate=cost(10**6, 2 * 10**6),
        name="inner",
    )(v, xt, gain)


def grad_in_kernel(v_ref, xt_ref, cot_ref, inv_ref, mean_ref, gain_ref, out_ref, scr):
    inv = inv_ref[...]
    scale = inv * inv * inv * mean_ref[...]

    def one(g, _):
        for i in range(NCH):
            c = i * SEQ + g
            u = gain_ref[c] * inv * v_ref[g, i].astype(F32) - scale * xt_ref[g, i].astype(F32)
            scr[pl.ds(pl.multiple_of(c * LOCAL, LOCAL), LOCAL), :] = u
        return 0

    lax.fori_loop(0, SEQ, one, 0)

    def two(m, _):
        r = pl.multiple_of(m * LANES, LANES)
        u = scr[pl.ds((m % 4) * 8 + m // 4, LANES, stride=LOCAL), :].T
        out_ref[pl.ds(r, LANES), :] = (cot_ref[pl.ds(r, LANES), :].astype(F32) + u).astype(BF16)
        return 0

    lax.fori_loop(0, LOCAL, two, 0)


def grad_in_of(v, xt, cot, inv, mean, gain):
    return pl.pallas_call(
        grad_in_kernel,
        out_shape=jax.ShapeDtypeStruct((LOCAL * LANES, LANES), BF16),
        in_specs=[vspec()] * 5 + [sspec()],
        out_specs=vspec(),
        scratch_shapes=[VMEM((LOCAL * LANES, LANES), F32)],
        compiler_params=params(),
        cost_estimate=cost(10**7, 5 * 10**6),
        name="grad_in",
    )(v, xt, cot, inv, mean, gain)


def exchange(a, axes):
    return lax.all_to_all(a, axes, 0, 0, tiled=True)


def sum_over_ch(a):
    total = a
    for by in (1, 2, 3):
        total = total + lax.ppermute(a, "ch", [(j, (j + by) % ZN) for j in range(ZN)])
    return total


def quarters(a):
    return a.reshape(8, ZN, LANES, LANES).swapaxes(0, 1).reshape(ZN, ROWS, LANES)


def own_channels(a, g):
    return lax.dynamic_index_in_dim(a.reshape(a.shape[:-1] + (NCH, SEQ)), g, a.ndim, False)


def level_weights(low, high, gain):
    low0, low1 = low[:, 0], low[:, 1]
    high0, high1 = high[:, 0], high[:, 1]
    ratio = gain[:LEVELS] * high1 / low1
    zero = jnp.zeros_like(ratio[:1])
    weight = jnp.concatenate([gain[:LEVELS] * high0 - ratio * low0, gain[LEVELS:]], axis=0)
    weight = weight + jnp.concatenate([zero, ratio], axis=0)
    scale = [jnp.ones_like(low0[0])]
    for k in range(LEVELS):
        scale.append(scale[-1] * low0[k])
    return (low1 / low0).reshape(-1), (weight * jnp.stack(scale)).reshape(-1)


def per_device(tokens, norm_gain, low_taps, high_taps, level_gain, mixing, lengths, cotangent):
    both = ("seq", "ch")
    g = lax.axis_index("seq")
    full = mixing.shape[0]
    bases = LOCAL * LANES * SEQ

    xt, squares = turn(tokens)
    x_seq = exchange(xt, "seq")
    cot_rows = exchange(quarters(cotangent), "ch")
    x_rows = exchange(quarters(tokens), "ch")
    inv = lax.rsqrt(sum_over_ch(squares) / full + EPS)
    inv_seq = exchange(jnp.broadcast_to(inv[None], (SEQ, LOCAL, LANES)), "seq")
    rel = rel_of(lengths)
    coef, weight = level_weights(
        own_channels(low_taps, g), own_channels(high_taps, g), own_channels(level_gain, g)
    )
    gh_seq = exchange(grad_hidden_of(cot_rows, mixing), both).reshape(SEQ, ZN, 32, LANES)
    hid, slope = forward(x_seq, inv_seq, rel, coef, weight, own_channels(norm_gain, g))
    hid_rows = exchange(hid.reshape(SEQ * ZN, 32, LANES), both)
    v = exchange(backward(gh_seq, slope, rel, coef, weight), "seq")
    out_rows, wg = mix(hid_rows, cot_rows, x_rows, mixing)
    layer_out = exchange(out_rows, "ch").reshape(ZN, 8, LANES, LANES).swapaxes(0, 1)
    layer_out = layer_out.reshape(LOCAL * LANES, LANES)
    weight_grad = jnp.sum(exchange(wg, both), axis=0).T / math.sqrt(bases)
    mean = sum_over_ch(inner(v, xt, norm_gain)) / full
    grad_in = grad_in_of(v, xt, cotangent, inv, mean, norm_gain)
    return (layer_out, grad_in, weight_grad)


def solution(mesh):
    in_specs = (
        P("seq", "ch"),
        P("ch"),
        P(None, None, "ch"),
        P(None, None, "ch"),
        P(None, "ch"),
        P(),
        P(),
        P("seq", "ch"),
    )
    out_specs = (P("seq", "ch"), P("seq", "ch"), P("ch", "seq"))
    return jax.shard_map(
        per_device, mesh=mesh, in_specs=in_specs, out_specs=out_specs, check_vma=False
    )
```

```python
import functools
import math

import jax
import jax.numpy as jnp
from jax import lax
from jax.experimental import pallas as pl
from jax.experimental.pallas import tpu as pltpu
from jax.sharding import PartitionSpec as P

LEVELS = 15
LANES = 128
NCH = 4
SEQ = 32
ZN = 4
ROWS = 1024
LOCAL = 32
FWD = 4
BWD = 4
EPS = 1e-06
F32 = jnp.float32
BF16 = jnp.bfloat16
VMEM = pltpu.VMEM
SMEM = pltpu.SMEM


def params():
    return pltpu.CompilerParams(vmem_limit_bytes=48 * 1024 * 1024)


def vspec():
    return pl.BlockSpec(memory_space=VMEM)


def sspec():
    return pl.BlockSpec(memory_space=SMEM)


def cost():
    return pl.CostEstimate(flops=1000, bytes_accessed=1000, transcendentals=0)


def turn_kernel(x_ref, xt_ref, scr):
    for m in range(LOCAL):
        j = m % 4 * 8 + m // 4
        t = x_ref[m * LANES : (m + 1) * LANES, :].astype(F32).T
        scr[j * LANES : (j + 1) * LANES, :] = t
    for g in range(SEQ):
        for i in range(NCH):
            xt_ref[g, i] = scr[pl.ds(i * SEQ + g, LOCAL, stride=LANES), :].astype(BF16)


def turn(x):
    return pl.pallas_call(
        turn_kernel,
        out_shape=jax.ShapeDtypeStruct((SEQ, NCH, LOCAL, LANES), BF16),
        in_specs=[vspec()],
        out_specs=vspec(),
        scratch_shapes=[VMEM((LOCAL * LANES, LANES), F32)],
        compiler_params=params(),
        cost_estimate=cost(),
        name="turn",
    )(x)


def rel_kernel(len_ref, rel_ref):
    starts = []
    at = jnp.int32(0)
    for n in range(15):
        at = at + len_ref[n]
        starts.append(at)
    shape = (4, 8, LANES)
    base = (
        lax.broadcasted_iota(jnp.int32, shape, 0) * LANES
        + lax.broadcasted_iota(jnp.int32, shape, 1) * 512
        + lax.broadcasted_iota(jnp.int32, shape, 2)
    )

    def one(s, _):
        t = base + s * (LOCAL * LANES)
        start = jnp.zeros(shape, jnp.int32)
        for n in range(15):
            start = jnp.where(t >= starts[n], starts[n], start)
        rel_ref[s] = t - start
        return 0

    lax.fori_loop(0, SEQ, one, 0)


def rel_of(lengths):
    return pl.pallas_call(
        rel_kernel,
        out_shape=jax.ShapeDtypeStruct((SEQ, 4, 8, LANES), jnp.int32),
        in_specs=[sspec()],
        out_specs=vspec(),
        compiler_params=params(),
        cost_estimate=cost(),
        name="rel",
    )(lengths)


def grad_hidden_kernel(me_ref, mix_ref, *refs):
    cot_refs, (out_ref, scr) = refs[:ZN], refs[ZN:]
    for m in range(8):
        acc = None
        for k in range(ZN):
            c = (me_ref[0] + ZN - k) % ZN
            part = lax.dot_general(
                mix_ref[:, pl.ds(pl.multiple_of(c * LANES, LANES), LANES)],
                cot_refs[k][m * LANES : (m + 1) * LANES, :],
                (((1,), (1,)), ((), ())),
                preferred_element_type=F32,
            )
            acc = part if acc is None else acc + part
        scr[m * 512 : (m + 1) * 512, :] = acc
    for g in range(SEQ):
        for c in range(ZN):
            rows = [scr[pl.ds(c * LANES + i * SEQ + g, 8, stride=512), :] for i in range(NCH)]
            out_ref[g * ZN + c] = jnp.concatenate(rows, axis=0).astype(BF16)


def grad_hidden_of(me, mixing, cot_parts):
    return pl.pallas_call(
        grad_hidden_kernel,
        out_shape=jax.ShapeDtypeStruct((SEQ * ZN, 32, LANES), BF16),
        in_specs=[sspec()] + [vspec()] * (1 + ZN),
        out_specs=vspec(),
        scratch_shapes=[VMEM((8 * 512, LANES), F32)],
        compiler_params=params(),
        cost_estimate=cost(),
        name="grad_hidden",
    )(me, mixing, *cot_parts)


def forward_kernel(FWD, x_ref, rel_ref, c_ref, w_ref, gain_ref, hid_ref, slope_ref, near, far):
    near[...] = jnp.zeros_like(near)
    far[...] = jnp.zeros_like(far)
    lane = lax.broadcasted_iota(jnp.int32, (8, LANES), 1)
    sub = lax.broadcasted_iota(jnp.int32, (8, LANES), 0)

    def before(now, old, by):
        return jnp.concatenate([old, now], axis=0)[old.shape[0] - by :][: now.shape[0]]

    def step(b, _):
        s = b * FWD
        rel = rel_ref[pl.ds(s, FWD)]
        inside = [rel >= 2**k for k in range(LEVELS)]
        inv = x_ref[pl.ds(s, FWD), NCH].astype(F32) + x_ref[pl.ds(s, FWD), NCH + 1].astype(F32)
        for pair in range(0, NCH, 2):
            hidden = []
            for i in (pair, pair + 1):
                z = x_ref[pl.ds(s, FWD), i].astype(F32) * (inv * gain_ref[i])
                z = z.reshape(FWD, 4, 8, LANES)
                y = w_ref[i] * z
                for k in range(LEVELS):
                    d = 2**k
                    if k < 8:
                        last = z[:, 3]
                        prev = before(last, near[k, i, pl.ds(3, 1)], 1)
                        near[k, i, pl.ds(3, 1)] = last[FWD - 1 :]
                        first = pltpu.roll(jnp.where(sub == 7, prev, last), 1, 1)
                        back = jnp.concatenate([first[:, None], z[:, :3]], axis=1)
                        if d < LANES:
                            back = pltpu.roll(jnp.where(lane >= LANES - d, back, z), d, 3)
                    elif k == 8:
                        last = z[:, 2:]
                        prev = before(last, near[k, i, pl.ds(2, 2)][None], 1)
                        near[k, i, pl.ds(2, 2)] = last[FWD - 1]
                        first = pltpu.roll(jnp.where(sub == 7, prev, last), 1, 2)
                        back = jnp.concatenate([first, z[:, :2]], axis=1)
                    elif k < 12:
                        by = 2 ** (k - 9)
                        prev = before(z, near[k, i][None], 1)
                        near[k, i] = z[FWD - 1]
                        back = pltpu.roll(jnp.where(sub >= 8 - by, prev, z), by, 2)
                    else:
                        by = 2 ** (k - 12)
                        old = far[k - 12, i]
                        back = before(z, old, by)
                        far[k - 12, i] = jnp.concatenate([old, z], axis=0)[FWD:]
                    z = z + c_ref[k * NCH + i] * jnp.where(inside[k], back, 0.0)
                    y = y + w_ref[(k + 1) * NCH + i] * z
                cdf = 0.5 * (1.0 + lax.erf(y * 0.7071067811865476))
                density = jnp.exp(-0.5 * y * y) * 0.3989422804014327
                slope_ref[i, pl.ds(s, FWD)] = cdf + y * density
                hidden.append(y * cdf)
            hid_ref[pl.ds(s, FWD), :, pl.ds(pair * 8, 16), :] = jnp.concatenate(
                hidden, axis=2
            ).astype(BF16)
        return 0

    lax.fori_loop(0, SEQ // FWD, step, 0)


def forward(x, rel, coef, weight, gain):
    return pl.pallas_call(
        functools.partial(forward_kernel, FWD),
        out_shape=(
            jax.ShapeDtypeStruct((SEQ, ZN, 32, LANES), BF16),
            jax.ShapeDtypeStruct((NCH, SEQ, 4, 8, LANES), F32),
        ),
        in_specs=[vspec(), vspec(), sspec(), sspec(), sspec()],
        out_specs=(vspec(), vspec()),
        scratch_shapes=[
            VMEM((12, NCH, 4, 8, LANES), F32),
            VMEM((3, NCH, 4, 4, 8, LANES), F32),
        ],
        compiler_params=params(),
        cost_estimate=cost(),
        name="forward",
    )(x, rel, coef, weight, gain)


def backward_kernel(BWD, gh_ref, slope_ref, rel_ref, c_ref, w_ref, out_ref, near, far):
    near[...] = jnp.zeros_like(near)
    far[...] = jnp.zeros_like(far)
    lane = lax.broadcasted_iota(jnp.int32, (8, LANES), 1)
    sub = lax.broadcasted_iota(jnp.int32, (8, LANES), 0)

    def after(now, old, by):
        return jnp.concatenate([now, old], axis=0)[by:][: now.shape[0]]

    def step(b, _):
        s = SEQ - BWD - b * BWD
        rel = rel_ref[pl.ds(s, BWD)]
        inside = [rel >= 2**k for k in range(LEVELS)]
        for pair in range(0, NCH, 2):
            block = gh_ref[pl.ds(s, BWD), :, pl.ds(pair * 8, 16), :].astype(F32)
            for i in (pair, pair + 1):
                grad = block[:, :, (i - pair) * 8 : (i - pair + 1) * 8]
                grad = grad * slope_ref[i, pl.ds(s, BWD)]
                v = w_ref[LEVELS * NCH + i] * grad
                for k in range(LEVELS - 1, -1, -1):
                    d = 2**k
                    p = jnp.where(inside[k], v, 0.0)
                    if k < 8:
                        head = p[:, 0]
                        foll = after(head, near[k, i, pl.ds(0, 1)], 1)
                        near[k, i, pl.ds(0, 1)] = head[:1]
                        end = pltpu.roll(jnp.where(sub == 0, foll, head), 7, 1)
                        ahead = jnp.concatenate([p[:, 1:], end[:, None]], axis=1)
                        if d < LANES:
                            ahead = pltpu.roll(jnp.where(lane < d, ahead, p), LANES - d, 3)
                    elif k == 8:
                        head = p[:, :2]
                        foll = after(head, near[k, i, pl.ds(0, 2)][None], 1)
                        near[k, i, pl.ds(0, 2)] = head[0]
                        end = pltpu.roll(jnp.where(sub == 0, foll, head), 7, 2)
                        ahead = jnp.concatenate([p[:, 2:], end], axis=1)
                    elif k < 12:
                        by = 2 ** (k - 9)
                        foll = after(p, near[k, i][None], 1)
                        near[k, i] = p[0]
                        ahead = pltpu.roll(jnp.where(sub < by, foll, p), 8 - by, 2)
                    else:
                        by = 2 ** (k - 12)
                        old = far[k - 12, i]
                        ahead = after(p, old, by)
                        far[k - 12, i] = jnp.concatenate([p, old], axis=0)[:4]
                    v = v + w_ref[k * NCH + i] * grad + c_ref[k * NCH + i] * ahead
                out_ref[pl.ds(s, BWD), i] = v.reshape(BWD, 32, LANES).astype(BF16)
        return 0

    lax.fori_loop(0, SEQ // BWD, step, 0)


def backward(gh, slope, rel, coef, weight):
    return pl.pallas_call(
        functools.partial(backward_kernel, BWD),
        out_shape=jax.ShapeDtypeStruct((SEQ, NCH, LOCAL, LANES), BF16),
        in_specs=[vspec(), vspec(), vspec(), sspec(), sspec()],
        out_specs=vspec(),
        scratch_shapes=[
            VMEM((12, NCH, 4, 8, LANES), F32),
            VMEM((3, NCH, 4, 4, 8, LANES), F32),
        ],
        compiler_params=params(),
        cost_estimate=cost(),
        name="backward",
    )(gh, slope, rel, coef, weight)


def mix_kernel(me_ref, hid_ref, mix_ref, *refs):
    cot_refs, x_refs, out_refs = refs[:ZN], refs[ZN : 2 * ZN], refs[2 * ZN : 3 * ZN]
    wg_refs, (scr, mixed, acc) = refs[3 * ZN : 4 * ZN], refs[4 * ZN :]
    column = [(me_ref[0] + ZN - k) % ZN for k in range(ZN)]

    def load(j, _):
        scr[pl.ds(pl.multiple_of(j * 128, 128), 128), :] = (
            hid_ref[pl.ds(j * 4, 4)].astype(F32).reshape(128, LANES)
        )
        return 0

    lax.fori_loop(0, SEQ, load, 0)

    for m in range(8):
        at = slice(m * LANES, (m + 1) * LANES)
        rows = [
            scr[pl.ds(c * 32 + i * 8 + m, SEQ, stride=LANES), :]
            for c in range(ZN)
            for i in range(NCH)
        ]
        h = jnp.concatenate(rows, axis=0)
        hb = h.astype(BF16)
        mixed[m % 2] = jnp.dot(h.T.astype(BF16), mix_ref[...], preferred_element_type=F32)
        for k in range(ZN):
            part = mixed[m % 2, :, pl.ds(pl.multiple_of(column[k] * LANES, LANES), LANES)]
            out_refs[k][at, :] = (x_refs[k][at, :].astype(F32) + part).astype(BF16)
            part = jnp.dot(hb, cot_refs[k][at, :], preferred_element_type=F32)
            acc[k] = part if m == 0 else acc[k] + part
    for k in range(ZN):
        row = pl.multiple_of((me_ref[0] + k) % ZN * LANES, LANES)
        for n in range(ZN):
            at = pl.ds(pl.multiple_of(column[n] * LANES, LANES), LANES)
            wg_refs[k][at, :] = acc[n, pl.ds(row, LANES), :].T


def mix(me, hid, mixing, cot_parts, x_parts):
    return pl.pallas_call(
        mix_kernel,
        out_shape=tuple(jax.ShapeDtypeStruct((ROWS, LANES), BF16) for _ in range(ZN))
        + tuple(jax.ShapeDtypeStruct((512, LANES), F32) for _ in range(ZN)),
        in_specs=[sspec()] + [vspec()] * (2 + 2 * ZN),
        out_specs=(vspec(),) * (2 * ZN),
        scratch_shapes=[
            VMEM((SEQ * ZN * 32, LANES), F32),
            VMEM((2, LANES, 512), F32),
            VMEM((ZN, 512, LANES), F32),
        ],
        compiler_params=params(),
        cost_estimate=cost(),
        name="mix",
    )(me, hid, mixing, *cot_parts, *x_parts)


def inner_kernel(v_ref, xt_ref, gain_ref, out_ref):
    def one(g, acc):
        for i in range(NCH):
            acc = acc + gain_ref[i * SEQ + g] * (v_ref[g, i].astype(F32) * xt_ref[g, i].astype(F32))
        return acc

    out_ref[...] = lax.fori_loop(0, SEQ, one, jnp.zeros((LOCAL, LANES), F32))


def inner(v, xt, gain):
    return pl.pallas_call(
        inner_kernel,
        out_shape=jax.ShapeDtypeStruct((LOCAL, LANES), F32),
        in_specs=[vspec(), vspec(), sspec()],
        out_specs=vspec(),
        compiler_params=params(),
        cost_estimate=cost(),
        name="inner",
    )(v, xt, gain)


def grad_in_kernel(v_ref, xt_ref, cot_ref, inv_ref, mean_ref, gain_ref, out_ref, scr):
    inv = inv_ref[...]
    scale = inv * inv * inv * mean_ref[...]

    for g in range(SEQ):
        for i in range(NCH):
            c = i * SEQ + g
            u = (gain_ref[c] * inv) * v_ref[g, i].astype(F32) - scale * xt_ref[g, i].astype(F32)
            scr[c * LOCAL : (c + 1) * LOCAL, :] = u
    for m in range(LOCAL):
        at = slice(m * LANES, (m + 1) * LANES)
        u = scr[pl.ds(m % 4 * 8 + m // 4, LANES, stride=LOCAL), :].T
        out_ref[at, :] = (cot_ref[at, :].astype(F32) + u).astype(BF16)


def grad_in_of(v, xt, cot, inv, mean, gain):
    return pl.pallas_call(
        grad_in_kernel,
        out_shape=jax.ShapeDtypeStruct((LOCAL * LANES, LANES), BF16),
        in_specs=[vspec()] * 5 + [sspec()],
        out_specs=vspec(),
        scratch_shapes=[VMEM((LOCAL * LANES, LANES), F32)],
        compiler_params=params(),
        cost_estimate=cost(),
        name="grad_in",
    )(v, xt, cot, inv, mean, gain)


def exchange(a, axes):
    return lax.all_to_all(a, axes, 0, 0, tiled=True)


def sum_over_ch(a):
    total = a
    for by in (1, 2, 3):
        total = total + turned(a, by)
    return total


def turned(a, by):
    return lax.ppermute(a, "ch", [(j, (j + by) % ZN) for j in range(ZN)]) if by else a


def parts_of(a, me):
    a = a.reshape(8, ZN, LANES, LANES)
    return [
        turned(
            lax.dynamic_index_in_dim(a, (me + k) % ZN, 1, False).reshape(ROWS, LANES), k
        )
        for k in range(ZN)
    ]


def whole_kernel(me_ref, *refs):
    parts, out_ref = refs[:ZN], refs[ZN]
    for k in range(ZN):
        r = (me_ref[0] + k) % ZN
        for n in range(8):
            out_ref[n, r] = parts[k][n * LANES : (n + 1) * LANES, :]


def whole_of(parts, place):
    return pl.pallas_call(
        whole_kernel,
        out_shape=jax.ShapeDtypeStruct((8, ZN, LANES, LANES), BF16),
        in_specs=[sspec()] + [vspec()] * ZN,
        out_specs=vspec(),
        compiler_params=params(),
        cost_estimate=cost(),
        name="whole",
    )(place, *parts).reshape(LOCAL * LANES, LANES)


def after(later, first):
    return lax.optimization_barrier((later, first))[0]


def own_channels(a, g):
    return lax.dynamic_index_in_dim(a.reshape(a.shape[:-1] + (NCH, SEQ)), g, a.ndim, False)


def level_weights(low, high, gain):
    low0, low1 = low[:, 0], low[:, 1]
    high0, high1 = high[:, 0], high[:, 1]
    ratio = gain[:LEVELS] * high1 / low1
    zero = jnp.zeros_like(ratio[:1])
    weight = jnp.concatenate([gain[:LEVELS] * high0 - ratio * low0, gain[LEVELS:]], axis=0)
    weight = weight + jnp.concatenate([zero, ratio], axis=0)
    scale = [jnp.ones_like(low0[0])]
    for k in range(LEVELS):
        scale.append(scale[-1] * low0[k])
    return (low1 / low0).reshape(-1), (weight * jnp.stack(scale)).reshape(-1)


def per_device(tokens, norm_gain, low_taps, high_taps, level_gain, mixing, lengths, cotangent):
    both = ("seq", "ch")
    g = lax.axis_index("seq")
    full = mixing.shape[0]
    bases = LOCAL * LANES * SEQ

    me = lax.axis_index("ch")
    place = me.reshape(1)

    x = tokens.astype(F32)
    squares = jnp.sum(x * x, axis=1).reshape(8, ZN, LANES).swapaxes(0, 1).reshape(LOCAL, LANES)
    inv = lax.rsqrt(sum_over_ch(squares) / full + EPS)
    inv_high = lax.reduce_precision(inv, 8, 7)
    inv_low = (inv - inv_high).astype(BF16)
    cot_parts = parts_of(after(cotangent, squares), me)
    xt = turn(tokens)
    sent = jnp.broadcast_to(
        jnp.stack([inv_high.astype(BF16), inv_low])[None], (SEQ, 2, LOCAL, LANES)
    )
    x_seq = exchange(jnp.concatenate([xt, sent], axis=1), "seq")
    rel = rel_of(lengths)
    coef, weight = level_weights(
        own_channels(low_taps, g), own_channels(high_taps, g), own_channels(level_gain, g)
    )
    gh = grad_hidden_of(after(place, (rel, coef, weight)), mixing, cot_parts)
    x_parts = parts_of(after(tokens, tuple(cot_parts[1:])), me)
    gh_seq = exchange(after(gh, (x_seq, x_parts)), both).reshape(SEQ, ZN, 32, LANES)
    hid, slope = forward(x_seq, rel, coef, weight, own_channels(norm_gain, g))
    hid_rows = exchange(after(hid, gh_seq).reshape(SEQ * ZN, 32, LANES), both)
    v = exchange(after(backward(gh_seq, slope, rel, coef, weight), hid_rows), "seq")
    mixed = mix(place, hid_rows, mixing, cot_parts, x_parts)
    wg = mixed[ZN]
    for k in range(1, ZN):
        wg = wg + turned(mixed[ZN + k], k)
    out_parts = [turned(after(mixed[k], wg), (ZN - k) % ZN) for k in range(ZN)]
    wg = exchange(after(wg, v).reshape(SEQ, 16, LANES), "seq")
    own = inner(v, xt, norm_gain)
    others, wg = lax.optimization_barrier(([turned(own, k) for k in range(1, ZN)], wg))
    mean = (own + others[0] + others[1] + others[2]) / full
    weight_grad = jnp.sum(wg, axis=0).T / math.sqrt(bases)
    grad_in = grad_in_of(v, xt, cotangent, inv, mean, norm_gain)
    layer_out = whole_of(out_parts, place)
    return (layer_out, grad_in, weight_grad)


def solution(mesh):
    in_specs = (
        P("seq", "ch"),
        P("ch"),
        P(None, None, "ch"),
        P(None, None, "ch"),
        P(None, "ch"),
        P(),
        P(),
        P("seq", "ch"),
    )
    out_specs = (P("seq", "ch"), P("seq", "ch"), P("ch", "seq"))
    return jax.shard_map(
        per_device, mesh=mesh, in_specs=in_specs, out_specs=out_specs, check_vma=False
    )
```

```python
import functools
import math

import jax
import jax.numpy as jnp
from jax import lax
from jax.experimental import pallas as pl
from jax.experimental.pallas import tpu as pltpu
from jax.sharding import PartitionSpec as P

LEVELS = 15
LANES = 128
NCH = 4
SEQ = 32
ZN = 4
ROWS = 1024
LOCAL = 32
FWD = 4
BWD = 4
EPS = 1e-06
SCALE = 2048.0
F32 = jnp.float32
BF16 = jnp.bfloat16
VMEM = pltpu.VMEM
SMEM = pltpu.SMEM


def params():
    return pltpu.CompilerParams(vmem_limit_bytes=16 * 1024 * 1024)


def vspec():
    return pl.BlockSpec(memory_space=VMEM)


def sspec():
    return pl.BlockSpec(memory_space=SMEM)


def cost():
    return pl.CostEstimate(flops=1000, bytes_accessed=1000, transcendentals=0)


def turn_kernel(x_ref, xt_ref, scr):
    for m in range(LOCAL):
        j = m % 4 * 8 + m // 4
        t = x_ref[m * LANES : (m + 1) * LANES, :].astype(F32).T
        scr[j * LANES : (j + 1) * LANES, :] = t
    for g in range(SEQ):
        for i in range(NCH):
            xt_ref[g, i] = scr[pl.ds(i * SEQ + g, LOCAL, stride=LANES), :].astype(BF16)


def turn(x):
    return pl.pallas_call(
        turn_kernel,
        out_shape=jax.ShapeDtypeStruct((SEQ, NCH, LOCAL, LANES), BF16),
        in_specs=[vspec()],
        out_specs=vspec(),
        scratch_shapes=[VMEM((LOCAL * LANES, LANES), F32)],
        compiler_params=params(),
        cost_estimate=cost(),
        name="turn",
    )(x)


def prepare_kernel(len_ref, low_ref, high_ref, level_ref, gain_ref, rel_ref, table_ref):
    starts = []
    at = jnp.int32(0)
    for n in range(15):
        at = at + len_ref[n]
        starts.append(at)
    shape = (4, 8, LANES)
    base = (
        lax.broadcasted_iota(jnp.int32, shape, 0) * LANES
        + lax.broadcasted_iota(jnp.int32, shape, 1) * 512
        + lax.broadcasted_iota(jnp.int32, shape, 2)
    )

    def one(s, _):
        t = base + s * (LOCAL * LANES)
        start = jnp.zeros(shape, jnp.int32)
        for n in range(15):
            start = jnp.where(t >= starts[n], starts[n], start)
        rel_ref[s] = t - start
        return 0

    lax.fori_loop(0, SEQ, one, 0)

    scale = jnp.ones((1, LANES), F32)
    carried = jnp.zeros((1, LANES), F32)
    for k in range(LEVELS):
        low0, low1 = low_ref[k, 0:1], low_ref[k, 1:2]
        gain = level_ref[k : k + 1]
        ratio = gain * high_ref[k, 1:2] / low1
        table_ref[k : k + 1] = low1 / low0
        table_ref[16 + k : 17 + k] = (gain * high_ref[k, 0:1] - ratio * low0 + carried) * scale
        scale = scale * low0
        carried = ratio
    table_ref[LEVELS : LEVELS + 1] = gain_ref[...]
    table_ref[31:32] = (level_ref[LEVELS : LEVELS + 1] + carried) * scale


def prepare(lengths, low, high, level_gain, gain):
    return pl.pallas_call(
        prepare_kernel,
        out_shape=(
            jax.ShapeDtypeStruct((SEQ, 4, 8, LANES), jnp.int32),
            jax.ShapeDtypeStruct((32, LANES), F32),
        ),
        in_specs=[sspec()] + [vspec()] * 4,
        out_specs=(vspec(), vspec()),
        compiler_params=params(),
        cost_estimate=cost(),
        name="prepare",
    )(lengths, low, high, level_gain, gain.reshape(1, LANES))


def grad_hidden_kernel(me_ref, mix_ref, *refs):
    cot_refs, (out_ref, held_ref, scr) = refs[:ZN], refs[ZN:]
    for k in range(ZN):
        c = (me_ref[0] + ZN - k) % ZN
        held_ref[k, :ROWS] = cot_refs[k][...]
        held_ref[k, ROWS:] = mix_ref[:, pl.ds(pl.multiple_of(c * LANES, LANES), LANES)]
    for m in range(8):
        acc = None
        for k in range(ZN):
            part = lax.dot_general(
                held_ref[k, ROWS:],
                held_ref[k, m * LANES : (m + 1) * LANES],
                (((1,), (1,)), ((), ())),
                preferred_element_type=F32,
            )
            acc = part if acc is None else acc + part
        scr[m * 512 : (m + 1) * 512, :] = acc
    for g in range(SEQ):
        for c in range(ZN):
            rows = [scr[pl.ds(c * LANES + i * SEQ + g, 8, stride=512), :] for i in range(NCH)]
            out_ref[g * ZN + c] = jnp.concatenate(rows, axis=0).astype(BF16)


def grad_hidden_of(me, mixing, cot_parts):
    return pl.pallas_call(
        grad_hidden_kernel,
        out_shape=(
            jax.ShapeDtypeStruct((SEQ * ZN, 32, LANES), BF16),
            jax.ShapeDtypeStruct((ZN, ROWS + 512, LANES), BF16),
        ),
        in_specs=[sspec()] + [vspec()] * (1 + ZN),
        out_specs=(vspec(), vspec()),
        scratch_shapes=[VMEM((8 * 512, LANES), F32)],
        compiler_params=params(),
        cost_estimate=cost(),
        name="grad_hidden",
    )(me, mixing, *cot_parts)


def forward_kernel(FWD, x_ref, rel_ref, t_ref, hid_ref, slope_ref, near, far):
    near[...] = jnp.zeros_like(near)
    far[...] = jnp.zeros_like(far)
    lane = lax.broadcasted_iota(jnp.int32, (8, LANES), 1)
    sub = lax.broadcasted_iota(jnp.int32, (8, LANES), 0)

    def before(now, old, by):
        return jnp.concatenate([old, now], axis=0)[old.shape[0] - by :][: now.shape[0]]

    def step(b, _):
        s = b * FWD
        rel = rel_ref[pl.ds(s, FWD)]
        inside = [rel >= 2**k for k in range(LEVELS)]
        for pair in range(0, NCH, 2):
            hidden = []
            for i in (pair, pair + 1):
                z = x_ref[pl.ds(s, FWD), i] * (t_ref[LEVELS * NCH + i] / SCALE)
                z = z.reshape(FWD, 4, 8, LANES)
                y = t_ref[16 * NCH + i] * z
                for k in range(LEVELS):
                    d = 2**k
                    if k < 8:
                        last = z[:, 3]
                        prev = before(last, near[k, i, pl.ds(3, 1)], 1)
                        near[k, i, pl.ds(3, 1)] = last[FWD - 1 :]
                        first = pltpu.roll(jnp.where(sub == 7, prev, last), 1, 1)
                        back = jnp.concatenate([first[:, None], z[:, :3]], axis=1)
                        if d < LANES:
                            back = pltpu.roll(jnp.where(lane >= LANES - d, back, z), d, 3)
                    elif k == 8:
                        last = z[:, 2:]
                        prev = before(last, near[k, i, pl.ds(2, 2)][None], 1)
                        near[k, i, pl.ds(2, 2)] = last[FWD - 1]
                        first = pltpu.roll(jnp.where(sub == 7, prev, last), 1, 2)
                        back = jnp.concatenate([first, z[:, :2]], axis=1)
                    elif k < 12:
                        by = 2 ** (k - 9)
                        prev = before(z, near[k, i][None], 1)
                        near[k, i] = z[FWD - 1]
                        back = pltpu.roll(jnp.where(sub >= 8 - by, prev, z), by, 2)
                    else:
                        by = 2 ** (k - 12)
                        old = far[k - 12, i]
                        back = before(z, old, by)
                        far[k - 12, i] = jnp.concatenate([old, z], axis=0)[FWD:]
                    z = z + t_ref[k * NCH + i] * jnp.where(inside[k], back, 0.0)
                    y = y + t_ref[(k + 17) * NCH + i] * z
                cdf = 0.5 * (1.0 + lax.erf(y * 0.7071067811865476))
                density = jnp.exp(-0.5 * y * y) * 0.3989422804014327
                slope_ref[i, pl.ds(s, FWD)] = cdf + y * density
                hidden.append(y * cdf)
            hid_ref[pl.ds(s, FWD), :, pl.ds(pair * 8, 16), :] = jnp.concatenate(
                hidden, axis=2
            ).astype(BF16)
        return 0

    lax.fori_loop(0, SEQ // FWD, step, 0)


def forward(x, rel, table):
    return pl.pallas_call(
        functools.partial(forward_kernel, FWD),
        out_shape=(
            jax.ShapeDtypeStruct((SEQ, ZN, 32, LANES), BF16),
            jax.ShapeDtypeStruct((NCH, SEQ, 4, 8, LANES), F32),
        ),
        in_specs=[vspec(), vspec(), sspec()],
        out_specs=(vspec(), vspec()),
        scratch_shapes=[
            VMEM((12, NCH, 4, 8, LANES), F32),
            VMEM((3, NCH, 4, 4, 8, LANES), F32),
        ],
        compiler_params=params(),
        cost_estimate=cost(),
        name="forward",
    )(x, rel, table)


def backward_kernel(BWD, gh_ref, slope_ref, rel_ref, t_ref, out_ref, near, far):
    near[...] = jnp.zeros_like(near)
    far[...] = jnp.zeros_like(far)
    lane = lax.broadcasted_iota(jnp.int32, (8, LANES), 1)
    sub = lax.broadcasted_iota(jnp.int32, (8, LANES), 0)

    def after(now, old, by):
        return jnp.concatenate([now, old], axis=0)[by:][: now.shape[0]]

    def step(b, _):
        s = SEQ - BWD - b * BWD
        rel = rel_ref[pl.ds(s, BWD)]
        inside = [rel >= 2**k for k in range(LEVELS)]
        for pair in range(0, NCH, 2):
            block = gh_ref[pl.ds(s, BWD), :, pl.ds(pair * 8, 16), :].astype(F32)
            for i in (pair, pair + 1):
                grad = block[:, :, (i - pair) * 8 : (i - pair + 1) * 8]
                grad = grad * slope_ref[i, pl.ds(s, BWD)]
                v = t_ref[31 * NCH + i] * grad
                for k in range(LEVELS - 1, -1, -1):
                    d = 2**k
                    p = jnp.where(inside[k], v, 0.0)
                    if k < 8:
                        head = p[:, 0]
                        foll = after(head, near[k, i, pl.ds(0, 1)], 1)
                        near[k, i, pl.ds(0, 1)] = head[:1]
                        end = pltpu.roll(jnp.where(sub == 0, foll, head), 7, 1)
                        ahead = jnp.concatenate([p[:, 1:], end[:, None]], axis=1)
                        if d < LANES:
                            ahead = pltpu.roll(jnp.where(lane < d, ahead, p), LANES - d, 3)
                    elif k == 8:
                        head = p[:, :2]
                        foll = after(head, near[k, i, pl.ds(0, 2)][None], 1)
                        near[k, i, pl.ds(0, 2)] = head[0]
                        end = pltpu.roll(jnp.where(sub == 0, foll, head), 7, 2)
                        ahead = jnp.concatenate([p[:, 2:], end], axis=1)
                    elif k < 12:
                        by = 2 ** (k - 9)
                        foll = after(p, near[k, i][None], 1)
                        near[k, i] = p[0]
                        ahead = pltpu.roll(jnp.where(sub < by, foll, p), 8 - by, 2)
                    else:
                        by = 2 ** (k - 12)
                        old = far[k - 12, i]
                        ahead = after(p, old, by)
                        far[k - 12, i] = jnp.concatenate([p, old], axis=0)[:4]
                    v = v + t_ref[(k + 16) * NCH + i] * grad + t_ref[k * NCH + i] * ahead
                out_ref[pl.ds(s, BWD), i] = v.reshape(BWD, 32, LANES).astype(BF16)
        return 0

    lax.fori_loop(0, SEQ // BWD, step, 0)


def backward(gh, slope, rel, table):
    return pl.pallas_call(
        functools.partial(backward_kernel, BWD),
        out_shape=jax.ShapeDtypeStruct((SEQ, NCH, LOCAL, LANES), BF16),
        in_specs=[vspec(), vspec(), vspec(), sspec()],
        out_specs=vspec(),
        scratch_shapes=[
            VMEM((12, NCH, 4, 8, LANES), F32),
            VMEM((3, NCH, 4, 4, 8, LANES), F32),
        ],
        compiler_params=params(),
        cost_estimate=cost(),
        name="backward",
    )(gh, slope, rel, table)


def mix_kernel(me_ref, hid_ref, held_ref, *refs):
    out_refs, wg_refs, (scr, acc) = refs[:ZN], refs[ZN : 2 * ZN], refs[2 * ZN :]

    def load(j, _):
        scr[pl.ds(pl.multiple_of(j * 128, 128), 128), :] = (
            hid_ref[pl.ds(j * 4, 4)].astype(F32).reshape(128, LANES)
        )
        return 0

    lax.fori_loop(0, SEQ, load, 0, unroll=4)

    for m in range(8):
        at = slice(m * LANES, (m + 1) * LANES)
        rows = [
            scr[pl.ds(c * 32 + i * 8 + m, SEQ, stride=LANES), :]
            for c in range(ZN)
            for i in range(NCH)
        ]
        h = jnp.concatenate(rows, axis=0)
        hb = h.astype(BF16)
        ht = h.T.astype(BF16)
        for k in range(ZN):
            part = jnp.dot(ht, held_ref[k, ROWS:], preferred_element_type=F32)
            out_refs[-k % ZN][at, :] = part.astype(BF16)
            part = jnp.dot(hb, held_ref[k, at], preferred_element_type=F32)
            acc[k] = part if m == 0 else acc[k] + part
    for n in range(ZN):
        row = pl.multiple_of((me_ref[0] + n) % ZN * LANES, LANES)
        for k in range(ZN):
            column = pl.multiple_of((me_ref[0] + ZN - k) % ZN * LANES, LANES)
            t = acc[k, pl.ds(row, LANES), :].T
            wg_refs[n][pl.ds(column, LANES), :] = t.astype(wg_refs[n].dtype)


def mix(me, hid, held):
    return pl.pallas_call(
        mix_kernel,
        out_shape=tuple(jax.ShapeDtypeStruct((ROWS, LANES), BF16) for _ in range(ZN))
        + tuple(jax.ShapeDtypeStruct((512, LANES), BF16 if n else F32) for n in range(ZN)),
        in_specs=[sspec(), vspec(), vspec()],
        out_specs=(vspec(),) * (2 * ZN),
        scratch_shapes=[
            VMEM((SEQ * ZN * 32, LANES), F32),
            VMEM((ZN, 512, LANES), F32),
        ],
        compiler_params=params(),
        cost_estimate=cost(),
        name="mix",
    )(me, hid, held)


def inner_kernel(v_ref, xt_ref, gain_ref, out_ref):
    def one(g, acc):
        for i in range(NCH):
            acc = acc + gain_ref[i * SEQ + g] * (v_ref[g, i].astype(F32) * xt_ref[g, i].astype(F32))
        return acc

    out_ref[...] = lax.fori_loop(0, SEQ, one, jnp.zeros((LOCAL, LANES), F32))


def inner(v, xt, gain):
    return pl.pallas_call(
        inner_kernel,
        out_shape=jax.ShapeDtypeStruct((LOCAL, LANES), F32),
        in_specs=[vspec(), vspec(), sspec()],
        out_specs=vspec(),
        compiler_params=params(),
        cost_estimate=cost(),
        name="inner",
    )(v, xt, gain)


def grad_in_kernel(v_ref, xt_ref, cot_ref, inv_ref, mean_ref, gain_ref, out_ref, scr):
    inv = inv_ref[...]
    scale = inv * inv * inv * mean_ref[...]

    for g in range(SEQ):
        for i in range(NCH):
            c = i * SEQ + g
            u = (gain_ref[c] * inv) * v_ref[g, i].astype(F32) - scale * xt_ref[g, i].astype(F32)
            scr[c * LOCAL : (c + 1) * LOCAL, :] = u
    for m in range(LOCAL):
        at = slice(m * LANES, (m + 1) * LANES)
        u = scr[pl.ds(m % 4 * 8 + m // 4, LANES, stride=LOCAL), :].T
        out_ref[at, :] = (cot_ref[at, :].astype(F32) + u).astype(BF16)


def grad_in_of(v, xt, cot, inv, mean, gain):
    return pl.pallas_call(
        grad_in_kernel,
        out_shape=jax.ShapeDtypeStruct((LOCAL * LANES, LANES), BF16),
        in_specs=[vspec()] * 5 + [sspec()],
        out_specs=vspec(),
        scratch_shapes=[VMEM((LOCAL * LANES, LANES), F32)],
        compiler_params=params(),
        cost_estimate=cost(),
        name="grad_in",
    )(v, xt, cot, inv, mean, gain)


def exchange(a, axes):
    return lax.all_to_all(a, axes, 0, 0, tiled=True)


def sum_over_ch(a):
    total = a
    for by in (1, 2, 3):
        total = total + turned(a, by)
    return total


def turned(a, by):
    return lax.ppermute(a, "ch", [(j, (j + by) % ZN) for j in range(ZN)]) if by else a


def parts_of(a, me):
    a = a.reshape(8, ZN, LANES, LANES)
    return [
        turned(
            lax.dynamic_index_in_dim(a, (me + k) % ZN, 1, False).reshape(ROWS, LANES), k
        )
        for k in range(ZN)
    ]


def whole_kernel(me_ref, x_ref, *refs):
    parts, out_ref = refs[:ZN], refs[ZN]
    for k in range(ZN):
        r = (me_ref[0] + ZN - k) % ZN
        for n in range(8):
            part = parts[k][n * LANES : (n + 1) * LANES, :].astype(F32)
            out_ref[n, r] = (x_ref[n, r].astype(F32) + part).astype(BF16)


def whole_of(x, parts, place):
    shape = (8, ZN, LANES, LANES)
    return pl.pallas_call(
        whole_kernel,
        out_shape=jax.ShapeDtypeStruct(shape, BF16),
        in_specs=[sspec()] + [vspec()] * (1 + ZN),
        out_specs=vspec(),
        compiler_params=params(),
        cost_estimate=cost(),
        name="whole",
    )(place, x.reshape(shape), *parts).reshape(LOCAL * LANES, LANES)


def after(later, first):
    return lax.optimization_barrier((later, first))[0]


def per_device(tokens, norm_gain, low_taps, high_taps, level_gain, mixing, lengths, cotangent):
    both = ("seq", "ch")
    g = lax.axis_index("seq")
    full = mixing.shape[0]
    bases = LOCAL * LANES * SEQ

    me = lax.axis_index("ch")
    place = me.reshape(1)

    x = tokens.astype(F32)
    squares = jnp.sum(x * x, axis=1).reshape(8, ZN, LANES).swapaxes(0, 1).reshape(LOCAL, LANES)
    inv = lax.rsqrt(sum_over_ch(squares) / full + EPS)
    cot_parts = parts_of(after(cotangent, squares), me)
    xt = turn(tokens)
    x_sent = (xt.astype(F32) * (inv * SCALE)).astype(jnp.float16)
    x_sent = exchange(x_sent, "seq")
    x_seq = x_sent.astype(F32)
    rel, table = prepare(lengths, low_taps, high_taps, level_gain, norm_gain)
    table = lax.dynamic_index_in_dim(table.reshape(32, NCH, SEQ), g, 2, False).reshape(-1)
    gh, held = grad_hidden_of(after(place, table), mixing, cot_parts)
    gh_seq = exchange(after(gh, x_sent), both).reshape(SEQ, ZN, 32, LANES)
    hid, slope = forward(x_seq, rel, table)
    hid_rows = exchange(after(hid, gh_seq).reshape(SEQ * ZN, 32, LANES), both)
    v = exchange(after(backward(gh_seq, slope, rel, table), hid_rows), "seq")
    mixed = mix(place, hid_rows, held)
    shares = [turned(mixed[ZN + n], n).astype(F32) for n in range(ZN)]
    wg = shares[0] + shares[1] + shares[2] + shares[3]
    parts = [turned(after(mixed[n], shares[1]), n) for n in range(ZN)]
    own = inner(v, xt, norm_gain)
    wg = exchange(after(wg, own).reshape(SEQ, 16, LANES), "seq")
    others, wg = lax.optimization_barrier(([turned(own, k) for k in range(1, ZN)], wg))
    mean = (own + others[0] + others[1] + others[2]) / full
    weight_grad = jnp.sum(wg, axis=0).T / math.sqrt(bases)
    grad_in = grad_in_of(v, xt, cotangent, inv, mean, norm_gain)
    layer_out = whole_of(tokens, parts, place)
    return (layer_out, grad_in, weight_grad)


def solution(mesh):
    in_specs = (
        P("seq", "ch"),
        P("ch"),
        P(None, None, "ch"),
        P(None, None, "ch"),
        P(None, "ch"),
        P(),
        P(),
        P("seq", "ch"),
    )
    out_specs = (P("seq", "ch"), P("seq", "ch"), P("ch", "seq"))
    return jax.shard_map(
        per_device, mesh=mesh, in_specs=in_specs, out_specs=out_specs, check_vma=False
    )
```

```python
import functools
import math

import jax
import jax.numpy as jnp
from jax import lax
from jax.experimental import pallas as pl
from jax.experimental.pallas import tpu as pltpu
from jax.sharding import PartitionSpec as P

LEVELS = 15
LANES = 128
NCH = 4
SEQ = 32
ZN = 4
ROWS = 1024
LOCAL = 32
FWD = 4
BWD = 4
EPS = 1e-06
SCALE = 2048.0
F32 = jnp.float32
BF16 = jnp.bfloat16
VMEM = pltpu.VMEM
SMEM = pltpu.SMEM


def params():
    return pltpu.CompilerParams(vmem_limit_bytes=16 * 1024 * 1024)


def vspec():
    return pl.BlockSpec(memory_space=VMEM)


def sspec():
    return pl.BlockSpec(memory_space=SMEM)


def cost():
    return pl.CostEstimate(flops=1000, bytes_accessed=1000, transcendentals=0)


def turn_kernel(x_ref, xt_ref, scr):
    for m in range(LOCAL):
        j = m % 4 * 8 + m // 4
        t = x_ref[m * LANES : (m + 1) * LANES, :].astype(F32).T
        scr[j * LANES : (j + 1) * LANES, :] = t
    for g in range(SEQ):
        for i in range(NCH):
            xt_ref[g, i] = scr[pl.ds(i * SEQ + g, LOCAL, stride=LANES), :].astype(BF16)


def turn(x):
    return pl.pallas_call(
        turn_kernel,
        out_shape=jax.ShapeDtypeStruct((SEQ, NCH, LOCAL, LANES), BF16),
        in_specs=[vspec()],
        out_specs=vspec(),
        scratch_shapes=[VMEM((LOCAL * LANES, LANES), F32)],
        compiler_params=params(),
        cost_estimate=cost(),
        name="turn",
    )(x)


def prepare_kernel(len_ref, low_ref, high_ref, level_ref, gain_ref, rel_ref, table_ref):
    starts = []
    at = jnp.int32(0)
    for n in range(15):
        at = at + len_ref[n]
        starts.append(at)
    shape = (4, 8, LANES)
    base = (
        lax.broadcasted_iota(jnp.int32, shape, 0) * LANES
        + lax.broadcasted_iota(jnp.int32, shape, 1) * 512
        + lax.broadcasted_iota(jnp.int32, shape, 2)
    )

    def one(s, _):
        t = base + s * (LOCAL * LANES)
        start = jnp.zeros(shape, jnp.int32)
        for n in range(15):
            start = jnp.where(t >= starts[n], starts[n], start)
        rel_ref[s] = t - start
        return 0

    lax.fori_loop(0, SEQ, one, 0)

    scale = jnp.ones((1, LANES), F32)
    carried = jnp.zeros((1, LANES), F32)
    for k in range(LEVELS):
        low0, low1 = low_ref[k, 0:1], low_ref[k, 1:2]
        gain = level_ref[k : k + 1]
        ratio = gain * high_ref[k, 1:2] / low1
        table_ref[k : k + 1] = low1 / low0
        table_ref[16 + k : 17 + k] = (gain * high_ref[k, 0:1] - ratio * low0 + carried) * scale
        scale = scale * low0
        carried = ratio
    table_ref[LEVELS : LEVELS + 1] = gain_ref[...]
    table_ref[31:32] = (level_ref[LEVELS : LEVELS + 1] + carried) * scale


def prepare(lengths, low, high, level_gain, gain):
    return pl.pallas_call(
        prepare_kernel,
        out_shape=(
            jax.ShapeDtypeStruct((SEQ, 4, 8, LANES), jnp.int32),
            jax.ShapeDtypeStruct((32, LANES), F32),
        ),
        in_specs=[sspec()] + [vspec()] * 4,
        out_specs=(vspec(), vspec()),
        compiler_params=params(),
        cost_estimate=cost(),
        name="prepare",
    )(lengths, low, high, level_gain, gain.reshape(1, LANES))


def grad_hidden_kernel(me_ref, mix_ref, *refs):
    cot_refs, (out_ref, held_ref, scr) = refs[:ZN], refs[ZN:]
    for k in range(ZN):
        held_ref[k] = cot_refs[k][...]
    for m in range(8):
        acc = None
        for k in range(ZN):
            c = (me_ref[0] + ZN - k) % ZN
            part = lax.dot_general(
                mix_ref[:, pl.ds(pl.multiple_of(c * LANES, LANES), LANES)],
                cot_refs[k][m * LANES : (m + 1) * LANES, :],
                (((1,), (1,)), ((), ())),
                preferred_element_type=F32,
            )
            acc = part if acc is None else acc + part
        scr[m * 512 : (m + 1) * 512, :] = acc
    for g in range(SEQ):
        for c in range(ZN):
            rows = [scr[pl.ds(c * LANES + i * SEQ + g, 8, stride=512), :] for i in range(NCH)]
            out_ref[g * ZN + c] = jnp.concatenate(rows, axis=0).astype(BF16)


def grad_hidden_of(me, mixing, cot_parts):
    return pl.pallas_call(
        grad_hidden_kernel,
        out_shape=(
            jax.ShapeDtypeStruct((SEQ * ZN, 32, LANES), BF16),
            jax.ShapeDtypeStruct((ZN, ROWS, LANES), BF16),
        ),
        in_specs=[sspec()] + [vspec()] * (1 + ZN),
        out_specs=(vspec(), vspec()),
        scratch_shapes=[VMEM((8 * 512, LANES), F32)],
        compiler_params=params(),
        cost_estimate=cost(),
        name="grad_hidden",
    )(me, mixing, *cot_parts)


def forward_kernel(FWD, x_ref, rel_ref, t_ref, hid_ref, slope_ref, near, far):
    near[...] = jnp.zeros_like(near)
    far[...] = jnp.zeros_like(far)
    lane = lax.broadcasted_iota(jnp.int32, (8, LANES), 1)
    sub = lax.broadcasted_iota(jnp.int32, (8, LANES), 0)

    def before(now, old, by):
        return jnp.concatenate([old, now], axis=0)[old.shape[0] - by :][: now.shape[0]]

    def step(b, _):
        s = b * FWD
        rel = rel_ref[pl.ds(s, FWD)]
        inside = [rel >= 2**k for k in range(LEVELS)]
        for pair in range(0, NCH, 2):
            hidden = []
            for i in (pair, pair + 1):
                z = x_ref[pl.ds(s, FWD), i] * (t_ref[LEVELS * NCH + i] / SCALE)
                z = z.reshape(FWD, 4, 8, LANES)
                y = t_ref[16 * NCH + i] * z
                for k in range(LEVELS):
                    d = 2**k
                    if k < 8:
                        last = z[:, 3]
                        prev = before(last, near[k, i, pl.ds(3, 1)], 1)
                        near[k, i, pl.ds(3, 1)] = last[FWD - 1 :]
                        first = pltpu.roll(jnp.where(sub == 7, prev, last), 1, 1)
                        back = jnp.concatenate([first[:, None], z[:, :3]], axis=1)
                        if d < LANES:
                            back = pltpu.roll(jnp.where(lane >= LANES - d, back, z), d, 3)
                    elif k == 8:
                        last = z[:, 2:]
                        prev = before(last, near[k, i, pl.ds(2, 2)][None], 1)
                        near[k, i, pl.ds(2, 2)] = last[FWD - 1]
                        first = pltpu.roll(jnp.where(sub == 7, prev, last), 1, 2)
                        back = jnp.concatenate([first, z[:, :2]], axis=1)
                    elif k < 12:
                        by = 2 ** (k - 9)
                        prev = before(z, near[k, i][None], 1)
                        near[k, i] = z[FWD - 1]
                        back = pltpu.roll(jnp.where(sub >= 8 - by, prev, z), by, 2)
                    else:
                        by = 2 ** (k - 12)
                        old = far[k - 12, i]
                        back = before(z, old, by)
                        far[k - 12, i] = jnp.concatenate([old, z], axis=0)[FWD:]
                    z = z + t_ref[k * NCH + i] * jnp.where(inside[k], back, 0.0)
                    y = y + t_ref[(k + 17) * NCH + i] * z
                cdf = 0.5 * (1.0 + lax.erf(y * 0.7071067811865476))
                density = jnp.exp(-0.5 * y * y) * 0.3989422804014327
                slope_ref[i, pl.ds(s, FWD)] = cdf + y * density
                hidden.append(y * cdf)
            hid_ref[pl.ds(s, FWD), :, pl.ds(pair * 8, 16), :] = jnp.concatenate(
                hidden, axis=2
            ).astype(BF16)
        return 0

    lax.fori_loop(0, SEQ // FWD, step, 0)


def forward(x, rel, table):
    return pl.pallas_call(
        functools.partial(forward_kernel, FWD),
        out_shape=(
            jax.ShapeDtypeStruct((SEQ, ZN, 32, LANES), BF16),
            jax.ShapeDtypeStruct((NCH, SEQ, 4, 8, LANES), F32),
        ),
        in_specs=[vspec(), vspec(), sspec()],
        out_specs=(vspec(), vspec()),
        scratch_shapes=[
            VMEM((12, NCH, 4, 8, LANES), F32),
            VMEM((3, NCH, 4, 4, 8, LANES), F32),
        ],
        compiler_params=params(),
        cost_estimate=cost(),
        name="forward",
    )(x, rel, table)


def backward_kernel(BWD, gh_ref, slope_ref, rel_ref, t_ref, out_ref, near, far):
    near[...] = jnp.zeros_like(near)
    far[...] = jnp.zeros_like(far)
    lane = lax.broadcasted_iota(jnp.int32, (8, LANES), 1)
    sub = lax.broadcasted_iota(jnp.int32, (8, LANES), 0)

    def after(now, old, by):
        return jnp.concatenate([now, old], axis=0)[by:][: now.shape[0]]

    def step(b, _):
        s = SEQ - BWD - b * BWD
        rel = rel_ref[pl.ds(s, BWD)]
        inside = [rel >= 2**k for k in range(LEVELS)]
        for pair in range(0, NCH, 2):
            block = gh_ref[pl.ds(s, BWD), :, pl.ds(pair * 8, 16), :].astype(F32)
            for i in (pair, pair + 1):
                grad = block[:, :, (i - pair) * 8 : (i - pair + 1) * 8]
                grad = grad * slope_ref[i, pl.ds(s, BWD)]
                v = t_ref[31 * NCH + i] * grad
                for k in range(LEVELS - 1, -1, -1):
                    d = 2**k
                    p = jnp.where(inside[k], v, 0.0)
                    if k < 8:
                        head = p[:, 0]
                        foll = after(head, near[k, i, pl.ds(0, 1)], 1)
                        near[k, i, pl.ds(0, 1)] = head[:1]
                        end = pltpu.roll(jnp.where(sub == 0, foll, head), 7, 1)
                        ahead = jnp.concatenate([p[:, 1:], end[:, None]], axis=1)
                        if d < LANES:
                            ahead = pltpu.roll(jnp.where(lane < d, ahead, p), LANES - d, 3)
                    elif k == 8:
                        head = p[:, :2]
                        foll = after(head, near[k, i, pl.ds(0, 2)][None], 1)
                        near[k, i, pl.ds(0, 2)] = head[0]
                        end = pltpu.roll(jnp.where(sub == 0, foll, head), 7, 2)
                        ahead = jnp.concatenate([p[:, 2:], end], axis=1)
                    elif k < 12:
                        by = 2 ** (k - 9)
                        foll = after(p, near[k, i][None], 1)
                        near[k, i] = p[0]
                        ahead = pltpu.roll(jnp.where(sub < by, foll, p), 8 - by, 2)
                    else:
                        by = 2 ** (k - 12)
                        old = far[k - 12, i]
                        ahead = after(p, old, by)
                        far[k - 12, i] = jnp.concatenate([p, old], axis=0)[:4]
                    v = v + t_ref[(k + 16) * NCH + i] * grad + t_ref[k * NCH + i] * ahead
                out_ref[pl.ds(s, BWD), i] = v.reshape(BWD, 32, LANES).astype(BF16)
        return 0

    lax.fori_loop(0, SEQ // BWD, step, 0)


def backward(gh, slope, rel, table):
    return pl.pallas_call(
        functools.partial(backward_kernel, BWD),
        out_shape=jax.ShapeDtypeStruct((SEQ, NCH, LOCAL, LANES), BF16),
        in_specs=[vspec(), vspec(), vspec(), sspec()],
        out_specs=vspec(),
        scratch_shapes=[
            VMEM((12, NCH, 4, 8, LANES), F32),
            VMEM((3, NCH, 4, 4, 8, LANES), F32),
        ],
        compiler_params=params(),
        cost_estimate=cost(),
        name="backward",
    )(gh, slope, rel, table)


def hidden_tiles(hid_ref, scr):
    def load(j, _):
        scr[pl.ds(pl.multiple_of(j * 128, 128), 128), :] = (
            hid_ref[pl.ds(j * 4, 4)].astype(F32).reshape(128, LANES)
        )
        return 0

    lax.fori_loop(0, SEQ, load, 0, unroll=4)
    for m in range(8):
        rows = [
            scr[pl.ds(c * 32 + i * 8 + m, SEQ, stride=LANES), :]
            for c in range(ZN)
            for i in range(NCH)
        ]
        yield m, slice(m * LANES, (m + 1) * LANES), jnp.concatenate(rows, axis=0)


def weigh_kernel(me_ref, hid_ref, held_ref, *refs):
    wg_refs, (scr, acc) = refs[:ZN], refs[ZN:]
    for m, at, h in hidden_tiles(hid_ref, scr):
        hb = h.astype(BF16)
        for k in range(ZN):
            part = jnp.dot(hb, held_ref[k, at], preferred_element_type=F32)
            acc[k] = part if m == 0 else acc[k] + part
    for n in range(ZN):
        row = pl.multiple_of((me_ref[0] + n) % ZN * LANES, LANES)
        for k in range(ZN):
            column = pl.multiple_of((me_ref[0] + ZN - k) % ZN * LANES, LANES)
            t = acc[k, pl.ds(row, LANES), :].T
            wg_refs[n][pl.ds(column, LANES), :] = t.astype(wg_refs[n].dtype)


def weigh(me, hid, held):
    return pl.pallas_call(
        weigh_kernel,
        out_shape=tuple(jax.ShapeDtypeStruct((512, LANES), BF16 if n else F32) for n in range(ZN)),
        in_specs=[sspec(), vspec(), vspec()],
        out_specs=(vspec(),) * ZN,
        scratch_shapes=[
            VMEM((SEQ * ZN * 32, LANES), F32),
            VMEM((ZN, 512, LANES), F32),
        ],
        compiler_params=params(),
        cost_estimate=cost(),
        name="weigh",
    )(me, hid, held)


def mix_kernel(me_ref, hid_ref, mix_ref, *refs):
    out_refs, scr = refs[:ZN], refs[ZN]
    for m, at, h in hidden_tiles(hid_ref, scr):
        ht = h.T.astype(BF16)
        for n in range(ZN):
            column = pl.ds(pl.multiple_of((me_ref[0] + n) % ZN * LANES, LANES), LANES)
            part = jnp.dot(ht, mix_ref[:, column], preferred_element_type=F32)
            out_refs[n][at, :] = part.astype(BF16)


def mix(me, hid, mixing):
    return pl.pallas_call(
        mix_kernel,
        out_shape=tuple(jax.ShapeDtypeStruct((ROWS, LANES), BF16) for _ in range(ZN)),
        in_specs=[sspec(), vspec(), vspec()],
        out_specs=(vspec(),) * ZN,
        scratch_shapes=[VMEM((SEQ * ZN * 32, LANES), F32)],
        compiler_params=params(),
        cost_estimate=cost(),
        name="mix",
    )(me, hid, mixing)


def inner_kernel(v_ref, xt_ref, gain_ref, out_ref):
    def one(g, acc):
        for i in range(NCH):
            acc = acc + gain_ref[i * SEQ + g] * (v_ref[g, i].astype(F32) * xt_ref[g, i].astype(F32))
        return acc

    out_ref[...] = lax.fori_loop(0, SEQ, one, jnp.zeros((LOCAL, LANES), F32))


def inner(v, xt, gain):
    return pl.pallas_call(
        inner_kernel,
        out_shape=jax.ShapeDtypeStruct((LOCAL, LANES), F32),
        in_specs=[vspec(), vspec(), sspec()],
        out_specs=vspec(),
        compiler_params=params(),
        cost_estimate=cost(),
        name="inner",
    )(v, xt, gain)


def grad_in_kernel(v_ref, xt_ref, cot_ref, inv_ref, mean_ref, gain_ref, out_ref, scr):
    inv = inv_ref[...]
    scale = inv * inv * inv * mean_ref[...]

    for g in range(SEQ):
        for i in range(NCH):
            c = i * SEQ + g
            u = (gain_ref[c] * inv) * v_ref[g, i].astype(F32) - scale * xt_ref[g, i].astype(F32)
            scr[c * LOCAL : (c + 1) * LOCAL, :] = u
    for m in range(LOCAL):
        at = slice(m * LANES, (m + 1) * LANES)
        u = scr[pl.ds(m % 4 * 8 + m // 4, LANES, stride=LOCAL), :].T
        out_ref[at, :] = (cot_ref[at, :].astype(F32) + u).astype(BF16)


def grad_in_of(v, xt, cot, inv, mean, gain):
    return pl.pallas_call(
        grad_in_kernel,
        out_shape=jax.ShapeDtypeStruct((LOCAL * LANES, LANES), BF16),
        in_specs=[vspec()] * 5 + [sspec()],
        out_specs=vspec(),
        scratch_shapes=[VMEM((LOCAL * LANES, LANES), F32)],
        compiler_params=params(),
        cost_estimate=cost(),
        name="grad_in",
    )(v, xt, cot, inv, mean, gain)


def exchange(a, axes):
    return lax.all_to_all(a, axes, 0, 0, tiled=True)


def sum_over_ch(a):
    total = a
    for by in (1, 2, 3):
        total = total + turned(a, by)
    return total


def turned(a, by):
    return lax.ppermute(a, "ch", [(j, (j + by) % ZN) for j in range(ZN)]) if by else a


def parts_of(a, me):
    a = a.reshape(8, ZN, LANES, LANES)
    return [
        turned(
            lax.dynamic_index_in_dim(a, (me + k) % ZN, 1, False).reshape(ROWS, LANES), k
        )
        for k in range(ZN)
    ]


def whole_kernel(me_ref, x_ref, *refs):
    parts, out_ref = refs[:ZN], refs[ZN]
    for k in range(ZN):
        r = (me_ref[0] + ZN - k) % ZN
        for n in range(8):
            part = parts[k][n * LANES : (n + 1) * LANES, :].astype(F32)
            out_ref[n, r] = (x_ref[n, r].astype(F32) + part).astype(BF16)


def whole_of(x, parts, place):
    shape = (8, ZN, LANES, LANES)
    return pl.pallas_call(
        whole_kernel,
        out_shape=jax.ShapeDtypeStruct(shape, BF16),
        in_specs=[sspec()] + [vspec()] * (1 + ZN),
        out_specs=vspec(),
        compiler_params=params(),
        cost_estimate=cost(),
        name="whole",
    )(place, x.reshape(shape), *parts).reshape(LOCAL * LANES, LANES)


def after(later, first):
    return lax.optimization_barrier((later, first))[0]


def per_device(tokens, norm_gain, low_taps, high_taps, level_gain, mixing, lengths, cotangent):
    both = ("seq", "ch")
    g = lax.axis_index("seq")
    full = mixing.shape[0]
    bases = LOCAL * LANES * SEQ

    me = lax.axis_index("ch")
    place = me.reshape(1)

    x = tokens.astype(F32)
    squares = jnp.sum(x * x, axis=1).reshape(8, ZN, LANES).swapaxes(0, 1).reshape(LOCAL, LANES)
    inv = lax.rsqrt(sum_over_ch(squares) / full + EPS)
    cot_parts = parts_of(after(cotangent, squares), me)
    xt = turn(tokens)
    x_sent = (xt.astype(F32) * (inv * SCALE)).astype(jnp.float16)
    x_sent = exchange(x_sent, "seq")
    x_seq = x_sent.astype(F32)
    rel, table = prepare(lengths, low_taps, high_taps, level_gain, norm_gain)
    table = lax.dynamic_index_in_dim(table.reshape(32, NCH, SEQ), g, 2, False).reshape(-1)
    gh, held = grad_hidden_of(after(place, table), mixing, cot_parts)
    gh_seq = exchange(after(gh, x_sent), both).reshape(SEQ, ZN, 32, LANES)
    hid, slope = forward(x_seq, rel, table)
    hid_rows = exchange(after(hid, gh_seq).reshape(SEQ * ZN, 32, LANES), both)
    v = exchange(after(backward(gh_seq, slope, rel, table), hid_rows), "seq")
    shares = weigh(place, hid_rows, held)
    own_first = shares[0]
    shares = [turned(shares[n], n).astype(F32) for n in range(ZN)]
    wg = shares[0] + shares[1] + shares[2] + shares[3]
    mixed = mix(after(place, own_first), hid_rows, mixing)
    parts = [turned(mixed[n], n) for n in range(ZN)]
    own = inner(v, xt, norm_gain)
    wg = exchange(after(wg, own).reshape(SEQ, 16, LANES), "seq")
    others = [turned(own, k) for k in range(1, ZN)]
    mean = (own + others[0] + others[1] + others[2]) / full
    grad_in = grad_in_of(v, xt, cotangent, inv, mean, norm_gain)
    weight_grad = jnp.sum(after(wg, grad_in), axis=0).T / math.sqrt(bases)
    layer_out = whole_of(tokens, parts, place)
    return (layer_out, grad_in, weight_grad)


def solution(mesh):
    in_specs = (
        P("seq", "ch"),
        P("ch"),
        P(None, None, "ch"),
        P(None, None, "ch"),
        P(None, "ch"),
        P(),
        P(),
        P("seq", "ch"),
    )
    out_specs = (P("seq", "ch"), P("seq", "ch"), P("ch", "seq"))
    return jax.shard_map(
        per_device, mesh=mesh, in_specs=in_specs, out_specs=out_specs, check_vma=False
    )
```

```python
import functools
import math

import jax
import jax.numpy as jnp
from jax import lax
from jax.experimental import pallas as pl
from jax.experimental.pallas import tpu as pltpu
from jax.sharding import PartitionSpec as P

LEVELS = 15
LANES = 128
NCH = 4
SEQ = 32
ZN = 4
ROWS = 1024
LOCAL = 32
FWD = 4
BWD = 4
EPS = 1e-06
GAP = 8
SCALE = 2048.0
F32 = jnp.float32
BF16 = jnp.bfloat16
VMEM = pltpu.VMEM
SMEM = pltpu.SMEM


def params():
    return pltpu.CompilerParams(vmem_limit_bytes=16 * 1024 * 1024)


def vspec():
    return pl.BlockSpec(memory_space=VMEM)


def sspec():
    return pl.BlockSpec(memory_space=SMEM)


def cost():
    return pl.CostEstimate(flops=1000, bytes_accessed=1000, transcendentals=0)


def turn_kernel(x_ref, xt_ref, scr):
    for m in range(LOCAL):
        j = m % 4 * 8 + m // 4
        t = x_ref[m * LANES : (m + 1) * LANES, :].astype(F32).T
        scr[j * (LANES + GAP) : j * (LANES + GAP) + LANES, :] = t
    for g in range(SEQ):
        for i in range(NCH):
            xt_ref[g, i] = scr[pl.ds(i * SEQ + g, LOCAL, stride=LANES + GAP), :].astype(BF16)


def turn(x):
    return pl.pallas_call(
        turn_kernel,
        out_shape=jax.ShapeDtypeStruct((SEQ, NCH, LOCAL, LANES), BF16),
        in_specs=[vspec()],
        out_specs=vspec(),
        scratch_shapes=[VMEM((LOCAL * (LANES + GAP), LANES), F32)],
        compiler_params=params(),
        cost_estimate=cost(),
        name="turn",
    )(x)


def prepare_kernel(len_ref, low_ref, high_ref, level_ref, gain_ref, rel_ref, table_ref):
    starts = []
    at = jnp.int32(0)
    for n in range(15):
        at = at + len_ref[n]
        starts.append(at)
    shape = (4, 8, LANES)
    base = (
        lax.broadcasted_iota(jnp.int32, shape, 0) * LANES
        + lax.broadcasted_iota(jnp.int32, shape, 1) * 512
        + lax.broadcasted_iota(jnp.int32, shape, 2)
    )

    def one(s, _):
        t = base + s * (LOCAL * LANES)
        start = jnp.zeros(shape, jnp.int32)
        for n in range(15):
            start = jnp.where(t >= starts[n], starts[n], start)
        rel_ref[s] = t - start
        return 0

    lax.fori_loop(0, SEQ, one, 0)

    scale = jnp.ones((1, LANES), F32)
    carried = jnp.zeros((1, LANES), F32)
    for k in range(LEVELS):
        low0, low1 = low_ref[k, 0:1], low_ref[k, 1:2]
        gain = level_ref[k : k + 1]
        ratio = gain * high_ref[k, 1:2] / low1
        table_ref[k : k + 1] = low1 / low0
        table_ref[16 + k : 17 + k] = (gain * high_ref[k, 0:1] - ratio * low0 + carried) * scale
        scale = scale * low0
        carried = ratio
    table_ref[LEVELS : LEVELS + 1] = gain_ref[...]
    table_ref[31:32] = (level_ref[LEVELS : LEVELS + 1] + carried) * scale


def prepare(lengths, low, high, level_gain, gain):
    return pl.pallas_call(
        prepare_kernel,
        out_shape=(
            jax.ShapeDtypeStruct((SEQ, 4, 8, LANES), jnp.int32),
            jax.ShapeDtypeStruct((32, LANES), F32),
        ),
        in_specs=[sspec()] + [vspec()] * 4,
        out_specs=(vspec(), vspec()),
        compiler_params=params(),
        cost_estimate=cost(),
        name="prepare",
    )(lengths, low, high, level_gain, gain.reshape(1, LANES))


def grad_hidden_kernel(me_ref, mix_ref, *refs):
    cot_refs, (out_ref, scr) = refs[:ZN], refs[ZN:]
    for m in range(8):
        acc = None
        for k in range(ZN):
            c = (me_ref[0] + ZN - k) % ZN
            part = lax.dot_general(
                mix_ref[:, pl.ds(pl.multiple_of(c * LANES, LANES), LANES)],
                cot_refs[k][m * LANES : (m + 1) * LANES, :],
                (((1,), (1,)), ((), ())),
                preferred_element_type=F32,
            )
            acc = part if acc is None else acc + part
        scr[m * (512 + GAP) : m * (512 + GAP) + 512, :] = acc
    for g in range(SEQ):
        for c in range(ZN):
            rows = [scr[pl.ds(c * LANES + i * SEQ + g, 8, stride=512 + GAP), :] for i in range(NCH)]
            out_ref[g * ZN + c] = jnp.concatenate(rows, axis=0).astype(BF16)


def grad_hidden_of(me, mixing, cot_parts):
    return pl.pallas_call(
        grad_hidden_kernel,
        out_shape=jax.ShapeDtypeStruct((SEQ * ZN, 32, LANES), BF16),
        in_specs=[sspec()] + [vspec()] * (1 + ZN),
        out_specs=vspec(),
        scratch_shapes=[VMEM((8 * (512 + GAP), LANES), F32)],
        compiler_params=params(),
        cost_estimate=cost(),
        name="grad_hidden",
    )(me, mixing, *cot_parts)


def forward_kernel(FWD, x_ref, rel_ref, t_ref, hid_ref, slope_ref, near, far):
    near[...] = jnp.zeros_like(near)
    far[...] = jnp.zeros_like(far)
    lane = lax.broadcasted_iota(jnp.int32, (8, LANES), 1)
    sub = lax.broadcasted_iota(jnp.int32, (8, LANES), 0)

    def before(now, old, by):
        return jnp.concatenate([old, now], axis=0)[old.shape[0] - by :][: now.shape[0]]

    def step(b, _):
        s = b * FWD
        rel = rel_ref[pl.ds(s, FWD)]
        inside = [rel >= 2**k for k in range(LEVELS)]
        for pair in range(0, NCH, 2):
            hidden = []
            for i in (pair, pair + 1):
                z = x_ref[pl.ds(s, FWD), i] * (t_ref[LEVELS * NCH + i] / SCALE)
                z = z.reshape(FWD, 4, 8, LANES)
                y = t_ref[16 * NCH + i] * z
                for k in range(LEVELS):
                    d = 2**k
                    if k < 8:
                        last = z[:, 3]
                        prev = before(last, near[k, i, pl.ds(3, 1)], 1)
                        near[k, i, pl.ds(3, 1)] = last[FWD - 1 :]
                        first = pltpu.roll(jnp.where(sub == 7, prev, last), 1, 1)
                        back = jnp.concatenate([first[:, None], z[:, :3]], axis=1)
                        if d < LANES:
                            back = pltpu.roll(jnp.where(lane >= LANES - d, back, z), d, 3)
                    elif k == 8:
                        last = z[:, 2:]
                        prev = before(last, near[k, i, pl.ds(2, 2)][None], 1)
                        near[k, i, pl.ds(2, 2)] = last[FWD - 1]
                        first = pltpu.roll(jnp.where(sub == 7, prev, last), 1, 2)
                        back = jnp.concatenate([first, z[:, :2]], axis=1)
                    elif k < 12:
                        by = 2 ** (k - 9)
                        prev = before(z, near[k, i][None], 1)
                        near[k, i] = z[FWD - 1]
                        back = pltpu.roll(jnp.where(sub >= 8 - by, prev, z), by, 2)
                    else:
                        by = 2 ** (k - 12)
                        old = far[k - 12, i]
                        back = before(z, old, by)
                        far[k - 12, i] = jnp.concatenate([old, z], axis=0)[FWD:]
                    z = z + t_ref[k * NCH + i] * jnp.where(inside[k], back, 0.0)
                    y = y + t_ref[(k + 17) * NCH + i] * z
                cdf = 0.5 * (1.0 + lax.erf(y * 0.7071067811865476))
                density = jnp.exp(-0.5 * y * y) * 0.3989422804014327
                slope_ref[i, pl.ds(s, FWD)] = cdf + y * density
                hidden.append(y * cdf)
            hid_ref[pl.ds(s, FWD), :, pl.ds(pair * 8, 16), :] = jnp.concatenate(
                hidden, axis=2
            ).astype(BF16)
        return 0

    lax.fori_loop(0, SEQ // FWD, step, 0)


def forward(x, rel, table):
    return pl.pallas_call(
        functools.partial(forward_kernel, FWD),
        out_shape=(
            jax.ShapeDtypeStruct((SEQ, ZN, 32, LANES), BF16),
            jax.ShapeDtypeStruct((NCH, SEQ, 4, 8, LANES), F32),
        ),
        in_specs=[vspec(), vspec(), sspec()],
        out_specs=(vspec(), vspec()),
        scratch_shapes=[
            VMEM((12, NCH, 4, 8, LANES), F32),
            VMEM((3, NCH, 4, 4, 8, LANES), F32),
        ],
        compiler_params=params(),
        cost_estimate=cost(),
        name="forward",
    )(x, rel, table)


def backward_kernel(BWD, gh_ref, slope_ref, rel_ref, t_ref, out_ref, near, far):
    near[...] = jnp.zeros_like(near)
    far[...] = jnp.zeros_like(far)
    lane = lax.broadcasted_iota(jnp.int32, (8, LANES), 1)
    sub = lax.broadcasted_iota(jnp.int32, (8, LANES), 0)

    def after(now, old, by):
        return jnp.concatenate([now, old], axis=0)[by:][: now.shape[0]]

    def step(b, _):
        s = SEQ - BWD - b * BWD
        rel = rel_ref[pl.ds(s, BWD)]
        inside = [rel >= 2**k for k in range(LEVELS)]
        for pair in range(0, NCH, 2):
            block = gh_ref[pl.ds(s, BWD), :, pl.ds(pair * 8, 16), :].astype(F32)
            for i in (pair, pair + 1):
                grad = block[:, :, (i - pair) * 8 : (i - pair + 1) * 8]
                grad = grad * slope_ref[i, pl.ds(s, BWD)]
                v = t_ref[31 * NCH + i] * grad
                for k in range(LEVELS - 1, -1, -1):
                    d = 2**k
                    p = jnp.where(inside[k], v, 0.0)
                    if k < 8:
                        head = p[:, 0]
                        foll = after(head, near[k, i, pl.ds(0, 1)], 1)
                        near[k, i, pl.ds(0, 1)] = head[:1]
                        end = pltpu.roll(jnp.where(sub == 0, foll, head), 7, 1)
                        ahead = jnp.concatenate([p[:, 1:], end[:, None]], axis=1)
                        if d < LANES:
                            ahead = pltpu.roll(jnp.where(lane < d, ahead, p), LANES - d, 3)
                    elif k == 8:
                        head = p[:, :2]
                        foll = after(head, near[k, i, pl.ds(0, 2)][None], 1)
                        near[k, i, pl.ds(0, 2)] = head[0]
                        end = pltpu.roll(jnp.where(sub == 0, foll, head), 7, 2)
                        ahead = jnp.concatenate([p[:, 2:], end], axis=1)
                    elif k < 12:
                        by = 2 ** (k - 9)
                        foll = after(p, near[k, i][None], 1)
                        near[k, i] = p[0]
                        ahead = pltpu.roll(jnp.where(sub < by, foll, p), 8 - by, 2)
                    else:
                        by = 2 ** (k - 12)
                        old = far[k - 12, i]
                        ahead = after(p, old, by)
                        far[k - 12, i] = jnp.concatenate([p, old], axis=0)[:4]
                    v = v + t_ref[(k + 16) * NCH + i] * grad + t_ref[k * NCH + i] * ahead
                out_ref[pl.ds(s, BWD), i] = v.reshape(BWD, 32, LANES).astype(BF16)
        return 0

    lax.fori_loop(0, SEQ // BWD, step, 0)


def backward(gh, slope, rel, table):
    return pl.pallas_call(
        functools.partial(backward_kernel, BWD),
        out_shape=jax.ShapeDtypeStruct((SEQ, NCH, LOCAL, LANES), BF16),
        in_specs=[vspec(), vspec(), vspec(), sspec()],
        out_specs=vspec(),
        scratch_shapes=[
            VMEM((12, NCH, 4, 8, LANES), F32),
            VMEM((3, NCH, 4, 4, 8, LANES), F32),
        ],
        compiler_params=params(),
        cost_estimate=cost(),
        name="backward",
    )(gh, slope, rel, table)


def hidden_tiles(hid_ref, scr):
    def load(j, _):
        scr[pl.ds(pl.multiple_of(j * (128 + GAP), 8), 128), :] = (
            hid_ref[pl.ds(j * 4, 4)].astype(F32).reshape(128, LANES)
        )
        return 0

    lax.fori_loop(0, SEQ, load, 0, unroll=4)
    for m in range(8):
        rows = [
            scr[pl.ds(c * 32 + i * 8 + m, SEQ, stride=LANES + GAP), :]
            for c in range(ZN)
            for i in range(NCH)
        ]
        yield m, slice(m * LANES, (m + 1) * LANES), jnp.concatenate(rows, axis=0)


def weigh_kernel(me_ref, hid_ref, held_ref, *refs):
    wg_refs, (scr, acc) = refs[:ZN], refs[ZN:]
    for m, at, h in hidden_tiles(hid_ref, scr):
        hb = h.astype(BF16)
        for k in range(ZN):
            part = jnp.dot(hb, held_ref[k, at], preferred_element_type=F32)
            acc[k] = part if m == 0 else acc[k] + part
    for n in range(ZN):
        row = pl.multiple_of((me_ref[0] + n) % ZN * LANES, LANES)
        for k in range(ZN):
            column = pl.multiple_of((me_ref[0] + ZN - k) % ZN * LANES, LANES)
            t = acc[k, pl.ds(row, LANES), :].T
            wg_refs[n][pl.ds(column, LANES), :] = t.astype(wg_refs[n].dtype)


def weigh(me, hid, held):
    return pl.pallas_call(
        weigh_kernel,
        out_shape=tuple(jax.ShapeDtypeStruct((512, LANES), BF16 if n else F32) for n in range(ZN)),
        in_specs=[sspec(), vspec(), vspec()],
        out_specs=(vspec(),) * ZN,
        scratch_shapes=[
            VMEM((SEQ * (LANES + GAP), LANES), F32),
            VMEM((ZN, 512, LANES), F32),
        ],
        compiler_params=params(),
        cost_estimate=cost(),
        name="weigh",
    )(me, hid, held)


def mix_kernel(me_ref, hid_ref, mix_ref, *refs):
    out_refs, scr = refs[:ZN], refs[ZN]
    for m, at, h in hidden_tiles(hid_ref, scr):
        ht = h.T.astype(BF16)
        for n in range(ZN):
            column = pl.ds(pl.multiple_of((me_ref[0] + n) % ZN * LANES, LANES), LANES)
            part = jnp.dot(ht, mix_ref[:, column], preferred_element_type=F32)
            out_refs[n][at, :] = part.astype(BF16)


def mix(me, hid, mixing):
    return pl.pallas_call(
        mix_kernel,
        out_shape=tuple(jax.ShapeDtypeStruct((ROWS, LANES), BF16) for _ in range(ZN)),
        in_specs=[sspec(), vspec(), vspec()],
        out_specs=(vspec(),) * ZN,
        scratch_shapes=[VMEM((SEQ * (LANES + GAP), LANES), F32)],
        compiler_params=params(),
        cost_estimate=cost(),
        name="mix",
    )(me, hid, mixing)


def inner_kernel(v_ref, xt_ref, gain_ref, out_ref):
    def one(g, acc):
        for i in range(NCH):
            acc = acc + gain_ref[i * SEQ + g] * (v_ref[g, i].astype(F32) * xt_ref[g, i].astype(F32))
        return acc

    out_ref[...] = lax.fori_loop(0, SEQ, one, jnp.zeros((LOCAL, LANES), F32))


def inner(v, xt, gain):
    return pl.pallas_call(
        inner_kernel,
        out_shape=jax.ShapeDtypeStruct((LOCAL, LANES), F32),
        in_specs=[vspec(), vspec(), sspec()],
        out_specs=vspec(),
        compiler_params=params(),
        cost_estimate=cost(),
        name="inner",
    )(v, xt, gain)


def grad_in_kernel(v_ref, xt_ref, cot_ref, inv_ref, mean_ref, gain_ref, out_ref, scr):
    inv = inv_ref[...]
    scale = inv * inv * inv * mean_ref[...]

    for g in range(SEQ):
        for i in range(NCH):
            c = i * SEQ + g
            u = (gain_ref[c] * inv) * v_ref[g, i].astype(F32) - scale * xt_ref[g, i].astype(F32)
            scr[c * (LOCAL + GAP) : c * (LOCAL + GAP) + LOCAL, :] = u
    for m in range(LOCAL):
        at = slice(m * LANES, (m + 1) * LANES)
        u = scr[pl.ds(m % 4 * 8 + m // 4, LANES, stride=LOCAL + GAP), :].T
        out_ref[at, :] = (cot_ref[at, :].astype(F32) + u).astype(BF16)


def grad_in_of(v, xt, cot, inv, mean, gain):
    return pl.pallas_call(
        grad_in_kernel,
        out_shape=jax.ShapeDtypeStruct((LOCAL * LANES, LANES), BF16),
        in_specs=[vspec()] * 5 + [sspec()],
        out_specs=vspec(),
        scratch_shapes=[VMEM((LANES * (LOCAL + GAP), LANES), F32)],
        compiler_params=params(),
        cost_estimate=cost(),
        name="grad_in",
    )(v, xt, cot, inv, mean, gain)


def exchange(a, axes):
    return lax.all_to_all(a, axes, 0, 0, tiled=True)


def sum_over_ch(a):
    total = a
    for by in (1, 2, 3):
        total = total + turned(a, by)
    return total


def turned(a, by):
    return lax.ppermute(a, "ch", [(j, (j + by) % ZN) for j in range(ZN)]) if by else a


def parts_of(a, me):
    a = a.reshape(8, ZN, LANES, LANES)
    return [
        turned(
            lax.dynamic_index_in_dim(a, (me + k) % ZN, 1, False).reshape(ROWS, LANES), k
        )
        for k in range(ZN)
    ]


def whole_kernel(me_ref, x_ref, *refs):
    parts, out_ref = refs[:ZN], refs[ZN]
    for k in range(ZN):
        r = (me_ref[0] + ZN - k) % ZN
        for n in range(8):
            part = parts[k][n * LANES : (n + 1) * LANES, :].astype(F32)
            out_ref[n, r] = (x_ref[n, r].astype(F32) + part).astype(BF16)


def whole_of(x, parts, place):
    shape = (8, ZN, LANES, LANES)
    return pl.pallas_call(
        whole_kernel,
        out_shape=jax.ShapeDtypeStruct(shape, BF16),
        in_specs=[sspec()] + [vspec()] * (1 + ZN),
        out_specs=vspec(),
        compiler_params=params(),
        cost_estimate=cost(),
        name="whole",
    )(place, x.reshape(shape), *parts).reshape(LOCAL * LANES, LANES)


def after(later, first):
    return lax.optimization_barrier((later, first))[0]


def per_device(tokens, norm_gain, low_taps, high_taps, level_gain, mixing, lengths, cotangent):
    both = ("seq", "ch")
    g = lax.axis_index("seq")
    full = mixing.shape[0]
    bases = LOCAL * LANES * SEQ

    me = lax.axis_index("ch")
    place = me.reshape(1)

    x = tokens.astype(F32)
    squares = jnp.sum(x * x, axis=1).reshape(8, ZN, LANES).swapaxes(0, 1).reshape(LOCAL, LANES)
    inv = lax.rsqrt(sum_over_ch(squares) / full + EPS)
    cot_parts = parts_of(after(cotangent, squares), me)
    xt = turn(tokens)
    x_sent = (xt.astype(F32) * (inv * SCALE)).astype(jnp.float16)
    x_sent = exchange(x_sent, "seq")
    x_seq = x_sent.astype(F32)
    rel, table = prepare(lengths, low_taps, high_taps, level_gain, norm_gain)
    table = lax.dynamic_index_in_dim(table.reshape(32, NCH, SEQ), g, 2, False).reshape(-1)
    gh = grad_hidden_of(after(place, table), mixing, cot_parts)
    gh_seq = exchange(after(gh, x_sent), both).reshape(SEQ, ZN, 32, LANES)
    held = jnp.stack(cot_parts)
    hid, slope = forward(x_seq, rel, table)
    hid_rows = exchange(after(hid, gh_seq).reshape(SEQ * ZN, 32, LANES), both)
    v = exchange(after(backward(gh_seq, after(slope, held), rel, table), hid_rows), "seq")
    shares = weigh(place, hid_rows, held)
    own_first = shares[0]
    shares = [turned(shares[n], n).astype(F32) for n in range(ZN)]
    wg = shares[0] + shares[1] + shares[2] + shares[3]
    mixed = mix(after(place, own_first), hid_rows, mixing)
    parts = [turned(mixed[n], n) for n in range(ZN)]
    own = inner(v, xt, norm_gain)
    wg = exchange(after(wg, own).reshape(SEQ, 16, LANES), "seq")
    others = [turned(own, k) for k in range(1, ZN)]
    mean = (own + others[0] + others[1] + others[2]) / full
    grad_in = grad_in_of(v, xt, cotangent, inv, mean, norm_gain)
    weight_grad = jnp.sum(after(wg, grad_in), axis=0).T / math.sqrt(bases)
    layer_out = whole_of(tokens, parts, place)
    return (layer_out, grad_in, weight_grad)


def solution(mesh):
    in_specs = (
        P("seq", "ch"),
        P("ch"),
        P(None, None, "ch"),
        P(None, None, "ch"),
        P(None, "ch"),
        P(),
        P(),
        P("seq", "ch"),
    )
    out_specs = (P("seq", "ch"), P("seq", "ch"), P("ch", "seq"))
    return jax.shard_map(
        per_device, mesh=mesh, in_specs=in_specs, out_specs=out_specs, check_vma=False
    )
```

```python
import functools
import math

import jax
import jax.numpy as jnp
from jax import lax
from jax.experimental import pallas as pl
from jax.experimental.pallas import tpu as pltpu
from jax.sharding import PartitionSpec as P

LEVELS = 15
LANES = 128
NCH = 4
SEQ = 32
ZN = 4
ROWS = 1024
LOCAL = 32
FWD = 4
BWD = 4
EPS = 1e-06
GAP = 8
SCALE = 2048.0
F32 = jnp.float32
BF16 = jnp.bfloat16
VMEM = pltpu.VMEM
SMEM = pltpu.SMEM


def params():
    return pltpu.CompilerParams(vmem_limit_bytes=16 * 1024 * 1024)


def vspec():
    return pl.BlockSpec(memory_space=VMEM)


def sspec():
    return pl.BlockSpec(memory_space=SMEM)


def cost():
    return pl.CostEstimate(flops=1000, bytes_accessed=1000, transcendentals=0)


def turn_kernel(x_ref, xt_ref, scr):
    for m in range(LOCAL):
        j = m % 4 * 8 + m // 4
        t = x_ref[m * LANES : (m + 1) * LANES, :].astype(F32).T
        scr[j * (LANES + GAP) : j * (LANES + GAP) + LANES, :] = t
    for g in range(SEQ):
        for i in range(NCH):
            xt_ref[g, i] = scr[pl.ds(i * SEQ + g, LOCAL, stride=LANES + GAP), :].astype(BF16)


def turn(x):
    return pl.pallas_call(
        turn_kernel,
        out_shape=jax.ShapeDtypeStruct((SEQ, NCH, LOCAL, LANES), BF16),
        in_specs=[vspec()],
        out_specs=vspec(),
        scratch_shapes=[VMEM((LOCAL * (LANES + GAP), LANES), F32)],
        compiler_params=params(),
        cost_estimate=cost(),
        name="turn",
    )(x)


def prepare_kernel(len_ref, low_ref, high_ref, level_ref, gain_ref, rel_ref, table_ref):
    starts = []
    at = jnp.int32(0)
    for n in range(15):
        at = at + len_ref[n]
        starts.append(at)
    shape = (4, 8, LANES)
    base = (
        lax.broadcasted_iota(jnp.int32, shape, 0) * LANES
        + lax.broadcasted_iota(jnp.int32, shape, 1) * 512
        + lax.broadcasted_iota(jnp.int32, shape, 2)
    )

    def one(s, _):
        t = base + s * (LOCAL * LANES)
        start = jnp.zeros(shape, jnp.int32)
        for n in range(15):
            start = jnp.where(t >= starts[n], starts[n], start)
        rel_ref[s] = t - start
        return 0

    lax.fori_loop(0, SEQ, one, 0)

    scale = jnp.ones((1, LANES), F32)
    carried = jnp.zeros((1, LANES), F32)
    for k in range(LEVELS):
        low0, low1 = low_ref[k, 0:1], low_ref[k, 1:2]
        gain = level_ref[k : k + 1]
        ratio = gain * high_ref[k, 1:2] / low1
        table_ref[k : k + 1] = low1 / low0
        table_ref[16 + k : 17 + k] = (gain * high_ref[k, 0:1] - ratio * low0 + carried) * scale
        scale = scale * low0
        carried = ratio
    table_ref[LEVELS : LEVELS + 1] = gain_ref[...]
    table_ref[31:32] = (level_ref[LEVELS : LEVELS + 1] + carried) * scale


def prepare(lengths, low, high, level_gain, gain):
    return pl.pallas_call(
        prepare_kernel,
        out_shape=(
            jax.ShapeDtypeStruct((SEQ, 4, 8, LANES), jnp.int32),
            jax.ShapeDtypeStruct((32, LANES), F32),
        ),
        in_specs=[sspec()] + [vspec()] * 4,
        out_specs=(vspec(), vspec()),
        compiler_params=params(),
        cost_estimate=cost(),
        name="prepare",
    )(lengths, low, high, level_gain, gain.reshape(1, LANES))


def grad_hidden_kernel(me_ref, mix_ref, *refs):
    cot_refs, (out_ref, scr) = refs[:ZN], refs[ZN:]
    columns = [
        pl.ds(pl.multiple_of((me_ref[0] + ZN - k) % ZN * LANES, LANES), LANES) for k in range(ZN)
    ]
    mixing = jnp.concatenate([mix_ref[:, column] for column in columns], axis=1)
    for m in range(0, 8, 2):
        rows = [cot_refs[k][m * LANES : (m + 2) * LANES, :] for k in range(ZN)]
        part = lax.dot_general(
            mixing,
            jnp.concatenate(rows, axis=1),
            (((1,), (1,)), ((), ())),
            preferred_element_type=F32,
        )
        for n in range(2):
            at = (m + n) * (512 + GAP)
            scr[at : at + 512, :] = part[:, n * LANES : (n + 1) * LANES]
    for g in range(SEQ):
        for c in range(ZN):
            rows = [scr[pl.ds(c * LANES + i * SEQ + g, 8, stride=512 + GAP), :] for i in range(NCH)]
            out_ref[g * ZN + c] = jnp.concatenate(rows, axis=0).astype(BF16)


def grad_hidden_of(me, mixing, cot_parts):
    return pl.pallas_call(
        grad_hidden_kernel,
        out_shape=jax.ShapeDtypeStruct((SEQ * ZN, 32, LANES), BF16),
        in_specs=[sspec()] + [vspec()] * (1 + ZN),
        out_specs=vspec(),
        scratch_shapes=[VMEM((8 * (512 + GAP), LANES), F32)],
        compiler_params=params(),
        cost_estimate=cost(),
        name="grad_hidden",
    )(me, mixing, *cot_parts)


def forward_kernel(FWD, x_ref, rel_ref, t_ref, hid_ref, slope_ref, near, far):
    near[...] = jnp.zeros_like(near)
    far[...] = jnp.zeros_like(far)
    lane = lax.broadcasted_iota(jnp.int32, (8, LANES), 1)
    sub = lax.broadcasted_iota(jnp.int32, (8, LANES), 0)

    def before(now, old, by):
        return jnp.concatenate([old, now], axis=0)[old.shape[0] - by :][: now.shape[0]]

    def step(b, _):
        s = b * FWD
        rel = rel_ref[pl.ds(s, FWD)]
        inside = [rel >= 2**k for k in range(LEVELS)]
        for pair in range(0, NCH, 2):
            hidden = []
            for i in (pair, pair + 1):
                z = x_ref[pl.ds(s, FWD), i] * (t_ref[LEVELS * NCH + i] / SCALE)
                z = z.reshape(FWD, 4, 8, LANES)
                y = t_ref[16 * NCH + i] * z
                for k in range(LEVELS):
                    d = 2**k
                    if k < 8:
                        last = z[:, 3]
                        prev = before(last, near[k, i, pl.ds(3, 1)], 1)
                        near[k, i, pl.ds(3, 1)] = last[FWD - 1 :]
                        first = pltpu.roll(jnp.where(sub == 7, prev, last), 1, 1)
                        back = jnp.concatenate([first[:, None], z[:, :3]], axis=1)
                        if d < LANES:
                            back = pltpu.roll(jnp.where(lane >= LANES - d, back, z), d, 3)
                    elif k == 8:
                        last = z[:, 2:]
                        prev = before(last, near[k, i, pl.ds(2, 2)][None], 1)
                        near[k, i, pl.ds(2, 2)] = last[FWD - 1]
                        first = pltpu.roll(jnp.where(sub == 7, prev, last), 1, 2)
                        back = jnp.concatenate([first, z[:, :2]], axis=1)
                    elif k < 12:
                        by = 2 ** (k - 9)
                        prev = before(z, near[k, i][None], 1)
                        near[k, i] = z[FWD - 1]
                        back = pltpu.roll(jnp.where(sub >= 8 - by, prev, z), by, 2)
                    else:
                        by = 2 ** (k - 12)
                        old = far[k - 12, i]
                        back = before(z, old, by)
                        far[k - 12, i] = jnp.concatenate([old, z], axis=0)[FWD:]
                    z = z + t_ref[k * NCH + i] * jnp.where(inside[k], back, 0.0)
                    y = y + t_ref[(k + 17) * NCH + i] * z
                cdf = 0.5 * (1.0 + lax.erf(y * 0.7071067811865476))
                density = jnp.exp(-0.5 * y * y) * 0.3989422804014327
                slope_ref[i, pl.ds(s, FWD)] = cdf + y * density
                hidden.append(y * cdf)
            hid_ref[pl.ds(s, FWD), :, pl.ds(pair * 8, 16), :] = jnp.concatenate(
                hidden, axis=2
            ).astype(BF16)
        return 0

    lax.fori_loop(0, SEQ // FWD, step, 0)


def forward(x, rel, table):
    return pl.pallas_call(
        functools.partial(forward_kernel, FWD),
        out_shape=(
            jax.ShapeDtypeStruct((SEQ, ZN, 32, LANES), BF16),
            jax.ShapeDtypeStruct((NCH, SEQ, 4, 8, LANES), F32),
        ),
        in_specs=[vspec(), vspec(), sspec()],
        out_specs=(vspec(), vspec()),
        scratch_shapes=[
            VMEM((12, NCH, 4, 8, LANES), F32),
            VMEM((3, NCH, 4, 4, 8, LANES), F32),
        ],
        compiler_params=params(),
        cost_estimate=cost(),
        name="forward",
    )(x, rel, table)


def backward_kernel(BWD, gh_ref, slope_ref, rel_ref, t_ref, out_ref, near, far):
    near[...] = jnp.zeros_like(near)
    far[...] = jnp.zeros_like(far)
    lane = lax.broadcasted_iota(jnp.int32, (8, LANES), 1)
    sub = lax.broadcasted_iota(jnp.int32, (8, LANES), 0)

    def after(now, old, by):
        return jnp.concatenate([now, old], axis=0)[by:][: now.shape[0]]

    def step(b, _):
        s = SEQ - BWD - b * BWD
        rel = rel_ref[pl.ds(s, BWD)]
        inside = [rel >= 2**k for k in range(LEVELS)]
        for pair in range(0, NCH, 2):
            block = gh_ref[pl.ds(s, BWD), :, pl.ds(pair * 8, 16), :].astype(F32)
            for i in (pair, pair + 1):
                grad = block[:, :, (i - pair) * 8 : (i - pair + 1) * 8]
                grad = grad * slope_ref[i, pl.ds(s, BWD)]
                v = t_ref[31 * NCH + i] * grad
                for k in range(LEVELS - 1, -1, -1):
                    d = 2**k
                    p = jnp.where(inside[k], v, 0.0)
                    if k < 8:
                        head = p[:, 0]
                        foll = after(head, near[k, i, pl.ds(0, 1)], 1)
                        near[k, i, pl.ds(0, 1)] = head[:1]
                        end = pltpu.roll(jnp.where(sub == 0, foll, head), 7, 1)
                        ahead = jnp.concatenate([p[:, 1:], end[:, None]], axis=1)
                        if d < LANES:
                            ahead = pltpu.roll(jnp.where(lane < d, ahead, p), LANES - d, 3)
                    elif k == 8:
                        head = p[:, :2]
                        foll = after(head, near[k, i, pl.ds(0, 2)][None], 1)
                        near[k, i, pl.ds(0, 2)] = head[0]
                        end = pltpu.roll(jnp.where(sub == 0, foll, head), 7, 2)
                        ahead = jnp.concatenate([p[:, 2:], end], axis=1)
                    elif k < 12:
                        by = 2 ** (k - 9)
                        foll = after(p, near[k, i][None], 1)
                        near[k, i] = p[0]
                        ahead = pltpu.roll(jnp.where(sub < by, foll, p), 8 - by, 2)
                    else:
                        by = 2 ** (k - 12)
                        old = far[k - 12, i]
                        ahead = after(p, old, by)
                        far[k - 12, i] = jnp.concatenate([p, old], axis=0)[:4]
                    v = v + t_ref[(k + 16) * NCH + i] * grad + t_ref[k * NCH + i] * ahead
                out_ref[pl.ds(s, BWD), i] = v.reshape(BWD, 32, LANES).astype(BF16)
        return 0

    lax.fori_loop(0, SEQ // BWD, step, 0)


def backward(gh, slope, rel, table):
    return pl.pallas_call(
        functools.partial(backward_kernel, BWD),
        out_shape=jax.ShapeDtypeStruct((SEQ, NCH, LOCAL, LANES), BF16),
        in_specs=[vspec(), vspec(), vspec(), sspec()],
        out_specs=vspec(),
        scratch_shapes=[
            VMEM((12, NCH, 4, 8, LANES), F32),
            VMEM((3, NCH, 4, 4, 8, LANES), F32),
        ],
        compiler_params=params(),
        cost_estimate=cost(),
        name="backward",
    )(gh, slope, rel, table)


def hidden_tiles(hid_ref, scr):
    def load(j, _):
        scr[pl.ds(pl.multiple_of(j * (128 + GAP), 8), 128), :] = (
            hid_ref[pl.ds(j * 4, 4)].astype(F32).reshape(128, LANES)
        )
        return 0

    lax.fori_loop(0, SEQ, load, 0, unroll=4)
    for m in range(8):
        rows = [
            scr[pl.ds(c * 32 + i * 8 + m, SEQ, stride=LANES + GAP), :]
            for c in range(ZN)
            for i in range(NCH)
        ]
        yield m, slice(m * LANES, (m + 1) * LANES), jnp.concatenate(rows, axis=0)


def weigh_kernel(me_ref, hid_ref, held_ref, *refs):
    wg_refs, (scr, acc) = refs[:ZN], refs[ZN:]
    for m, at, h in hidden_tiles(hid_ref, scr):
        hb = h.astype(BF16)
        rows = jnp.concatenate([held_ref[k, at] for k in range(ZN)], axis=1)
        part = jnp.dot(hb, rows, preferred_element_type=F32)
        acc[...] = part if m == 0 else acc[...] + part
    for n in range(ZN):
        row = pl.multiple_of((me_ref[0] + n) % ZN * LANES, LANES)
        for k in range(ZN):
            column = pl.multiple_of((me_ref[0] + ZN - k) % ZN * LANES, LANES)
            t = acc[pl.ds(row, LANES), k * LANES : (k + 1) * LANES].T
            wg_refs[n][pl.ds(column, LANES), :] = t.astype(wg_refs[n].dtype)


def weigh(me, hid, held):
    return pl.pallas_call(
        weigh_kernel,
        out_shape=tuple(jax.ShapeDtypeStruct((512, LANES), BF16 if n else F32) for n in range(ZN)),
        in_specs=[sspec(), vspec(), vspec()],
        out_specs=(vspec(),) * ZN,
        scratch_shapes=[
            VMEM((SEQ * (LANES + GAP), LANES), F32),
            VMEM((512, 512), F32),
        ],
        compiler_params=params(),
        cost_estimate=cost(),
        name="weigh",
    )(me, hid, held)


def mix_kernel(me_ref, hid_ref, mix_ref, *refs):
    out_refs, scr = refs[:ZN], refs[ZN]
    columns = [
        pl.ds(pl.multiple_of((me_ref[0] + n) % ZN * LANES, LANES), LANES) for n in range(ZN)
    ]
    mixing = jnp.concatenate([mix_ref[:, column] for column in columns], axis=1)
    for m, at, h in hidden_tiles(hid_ref, scr):
        mixed = jnp.dot(h.T.astype(BF16), mixing, preferred_element_type=F32)
        for n in range(ZN):
            out_refs[n][at, :] = mixed[:, n * LANES : (n + 1) * LANES].astype(BF16)


def mix(me, hid, mixing):
    return pl.pallas_call(
        mix_kernel,
        out_shape=tuple(jax.ShapeDtypeStruct((ROWS, LANES), BF16) for _ in range(ZN)),
        in_specs=[sspec(), vspec(), vspec()],
        out_specs=(vspec(),) * ZN,
        scratch_shapes=[VMEM((SEQ * (LANES + GAP), LANES), F32)],
        compiler_params=params(),
        cost_estimate=cost(),
        name="mix",
    )(me, hid, mixing)


def inner_kernel(v_ref, xt_ref, gain_ref, out_ref):
    def one(g, acc):
        for i in range(NCH):
            acc = acc + gain_ref[i * SEQ + g] * (v_ref[g, i].astype(F32) * xt_ref[g, i].astype(F32))
        return acc

    out_ref[...] = lax.fori_loop(0, SEQ, one, jnp.zeros((LOCAL, LANES), F32))


def inner(v, xt, gain):
    return pl.pallas_call(
        inner_kernel,
        out_shape=jax.ShapeDtypeStruct((LOCAL, LANES), F32),
        in_specs=[vspec(), vspec(), sspec()],
        out_specs=vspec(),
        compiler_params=params(),
        cost_estimate=cost(),
        name="inner",
    )(v, xt, gain)


def grad_in_kernel(v_ref, xt_ref, cot_ref, inv_ref, mean_ref, gain_ref, out_ref, scr):
    inv = inv_ref[...]
    scale = inv * inv * inv * mean_ref[...]

    for g in range(SEQ):
        for i in range(NCH):
            c = i * SEQ + g
            u = (gain_ref[c] * inv) * v_ref[g, i].astype(F32) - scale * xt_ref[g, i].astype(F32)
            scr[c * (LOCAL + GAP) : c * (LOCAL + GAP) + LOCAL, :] = u
    for m in range(LOCAL):
        at = slice(m * LANES, (m + 1) * LANES)
        u = scr[pl.ds(m % 4 * 8 + m // 4, LANES, stride=LOCAL + GAP), :].T
        out_ref[at, :] = (cot_ref[at, :].astype(F32) + u).astype(BF16)


def grad_in_of(v, xt, cot, inv, mean, gain):
    return pl.pallas_call(
        grad_in_kernel,
        out_shape=jax.ShapeDtypeStruct((LOCAL * LANES, LANES), BF16),
        in_specs=[vspec()] * 5 + [sspec()],
        out_specs=vspec(),
        scratch_shapes=[VMEM((LANES * (LOCAL + GAP), LANES), F32)],
        compiler_params=params(),
        cost_estimate=cost(),
        name="grad_in",
    )(v, xt, cot, inv, mean, gain)


def exchange(a, axes):
    return lax.all_to_all(a, axes, 0, 0, tiled=True)


def sum_over_ch(a):
    total = a
    for by in (1, 2, 3):
        total = total + turned(a, by)
    return total


def turned(a, by):
    return lax.ppermute(a, "ch", [(j, (j + by) % ZN) for j in range(ZN)]) if by else a


def parts_of(a, me):
    a = a.reshape(8, ZN, LANES, LANES)
    return [
        turned(
            lax.dynamic_index_in_dim(a, (me + k) % ZN, 1, False).reshape(ROWS, LANES), k
        )
        for k in range(ZN)
    ]


def whole_kernel(me_ref, x_ref, *refs):
    parts, out_ref = refs[:ZN], refs[ZN]
    for k in range(ZN):
        r = (me_ref[0] + ZN - k) % ZN
        for n in range(8):
            part = parts[k][n * LANES : (n + 1) * LANES, :].astype(F32)
            out_ref[n, r] = (x_ref[n, r].astype(F32) + part).astype(BF16)


def whole_of(x, parts, place):
    shape = (8, ZN, LANES, LANES)
    return pl.pallas_call(
        whole_kernel,
        out_shape=jax.ShapeDtypeStruct(shape, BF16),
        in_specs=[sspec()] + [vspec()] * (1 + ZN),
        out_specs=vspec(),
        compiler_params=params(),
        cost_estimate=cost(),
        name="whole",
    )(place, x.reshape(shape), *parts).reshape(LOCAL * LANES, LANES)


def after(later, first):
    return lax.optimization_barrier((later, first))[0]


def per_device(tokens, norm_gain, low_taps, high_taps, level_gain, mixing, lengths, cotangent):
    both = ("seq", "ch")
    g = lax.axis_index("seq")
    full = mixing.shape[0]
    bases = LOCAL * LANES * SEQ

    me = lax.axis_index("ch")
    place = me.reshape(1)

    x = tokens.astype(F32)
    squares = jnp.sum(x * x, axis=1).reshape(8, ZN, LANES).swapaxes(0, 1).reshape(LOCAL, LANES)
    inv = lax.rsqrt(sum_over_ch(squares) / full + EPS)
    cot_parts = parts_of(after(cotangent, squares), me)
    xt = turn(tokens)
    x_sent = (xt.astype(F32) * (inv * SCALE)).astype(jnp.float16)
    x_sent = exchange(x_sent, "seq")
    x_seq = x_sent.astype(F32)
    rel, table = prepare(lengths, low_taps, high_taps, level_gain, norm_gain)
    table = lax.dynamic_index_in_dim(table.reshape(32, NCH, SEQ), g, 2, False).reshape(-1)
    gh = grad_hidden_of(after(place, table), mixing, cot_parts)
    gh_seq = exchange(after(gh, x_sent), both).reshape(SEQ, ZN, 32, LANES)
    held = jnp.stack(cot_parts)
    hid, slope = forward(x_seq, rel, table)
    hid_rows = exchange(after(hid, gh_seq).reshape(SEQ * ZN, 32, LANES), both)
    v = exchange(after(backward(gh_seq, after(slope, held), rel, table), hid_rows), "seq")
    shares = weigh(place, hid_rows, held)
    own_first = shares[0]
    shares = [turned(shares[n], n).astype(F32) for n in range(ZN)]
    wg = (shares[0] + shares[1] + shares[2] + shares[3]) / math.sqrt(bases)
    mixed = mix(after(place, own_first), hid_rows, mixing)
    parts = [turned(mixed[n], n) for n in range(ZN)]
    own = inner(v, xt, norm_gain)
    wg = exchange(after(wg, own).reshape(SEQ, 16, LANES), "seq")
    others = [turned(own, k) for k in range(1, ZN)]
    mean = (own + others[0] + others[1] + others[2]) / full
    grad_in = grad_in_of(v, xt, cotangent, inv, mean, norm_gain)
    weight_grad = jnp.sum(after(wg, grad_in), axis=0).T
    layer_out = whole_of(tokens, parts, place)
    return (layer_out, grad_in, weight_grad)


def solution(mesh):
    in_specs = (
        P("seq", "ch"),
        P("ch"),
        P(None, None, "ch"),
        P(None, None, "ch"),
        P(None, "ch"),
        P(),
        P(),
        P("seq", "ch"),
    )
    out_specs = (P("seq", "ch"), P("seq", "ch"), P("ch", "seq"))
    return jax.shard_map(
        per_device, mesh=mesh, in_specs=in_specs, out_specs=out_specs, check_vma=False
    )
```

```python
import functools
import math

import jax
import jax.numpy as jnp
from jax import lax
from jax.experimental import pallas as pl
from jax.experimental.pallas import tpu as pltpu
from jax.sharding import PartitionSpec as P

LEVELS = 15
LANES = 128
NCH = 4
SEQ = 32
ZN = 4
ROWS = 1024
LOCAL = 32
FWD = 4
BWD = 4
EPS = 1e-06
GAP = 8
SCALE = 2048.0
F32 = jnp.float32
BF16 = jnp.bfloat16
VMEM = pltpu.VMEM
SMEM = pltpu.SMEM


def params():
    return pltpu.CompilerParams(vmem_limit_bytes=16 * 1024 * 1024)


def vspec():
    return pl.BlockSpec(memory_space=VMEM)


def sspec():
    return pl.BlockSpec(memory_space=SMEM)


def cost():
    return pl.CostEstimate(flops=1000, bytes_accessed=1000, transcendentals=0)


def turn_kernel(x_ref, xt_ref, scr):
    for m in range(LOCAL):
        j = m % 4 * 8 + m // 4
        t = x_ref[m * LANES : (m + 1) * LANES, :].astype(F32).T
        scr[j * (LANES + GAP) : j * (LANES + GAP) + LANES, :] = t
    for g in range(SEQ):
        for i in range(NCH):
            xt_ref[g, i] = scr[pl.ds(i * SEQ + g, LOCAL, stride=LANES + GAP), :].astype(BF16)


def turn(x):
    return pl.pallas_call(
        turn_kernel,
        out_shape=jax.ShapeDtypeStruct((SEQ, NCH, LOCAL, LANES), BF16),
        in_specs=[vspec()],
        out_specs=vspec(),
        scratch_shapes=[VMEM((LOCAL * (LANES + GAP), LANES), F32)],
        compiler_params=params(),
        cost_estimate=cost(),
        name="turn",
    )(x)


def prepare_kernel(len_ref, low_ref, high_ref, level_ref, gain_ref, rel_ref, table_ref):
    starts = []
    at = jnp.int32(0)
    for n in range(15):
        at = at + len_ref[n]
        starts.append(at)
    shape = (4, 8, LANES)
    base = (
        lax.broadcasted_iota(jnp.int32, shape, 0) * LANES
        + lax.broadcasted_iota(jnp.int32, shape, 1) * 512
        + lax.broadcasted_iota(jnp.int32, shape, 2)
    )

    def one(s, _):
        t = base + s * (LOCAL * LANES)
        start = jnp.zeros(shape, jnp.int32)
        for n in range(15):
            start = jnp.where(t >= starts[n], starts[n], start)
        rel_ref[s] = t - start
        return 0

    lax.fori_loop(0, SEQ, one, 0)

    scale = jnp.ones((1, LANES), F32)
    carried = jnp.zeros((1, LANES), F32)
    for k in range(LEVELS):
        low0, low1 = low_ref[k, 0:1], low_ref[k, 1:2]
        gain = level_ref[k : k + 1]
        ratio = gain * high_ref[k, 1:2] / low1
        table_ref[k : k + 1] = low1 / low0
        table_ref[16 + k : 17 + k] = (gain * high_ref[k, 0:1] - ratio * low0 + carried) * scale
        scale = scale * low0
        carried = ratio
    table_ref[LEVELS : LEVELS + 1] = gain_ref[...]
    table_ref[31:32] = (level_ref[LEVELS : LEVELS + 1] + carried) * scale


def prepare(lengths, low, high, level_gain, gain):
    return pl.pallas_call(
        prepare_kernel,
        out_shape=(
            jax.ShapeDtypeStruct((SEQ, 4, 8, LANES), jnp.int32),
            jax.ShapeDtypeStruct((32, LANES), F32),
        ),
        in_specs=[sspec()] + [vspec()] * 4,
        out_specs=(vspec(), vspec()),
        compiler_params=params(),
        cost_estimate=cost(),
        name="prepare",
    )(lengths, low, high, level_gain, gain.reshape(1, LANES))


def grad_hidden_kernel(me_ref, mix_ref, *refs):
    cot_refs, (out_ref, scr) = refs[:ZN], refs[ZN:]
    columns = [
        pl.ds(pl.multiple_of((me_ref[0] + ZN - k) % ZN * LANES, LANES), LANES) for k in range(ZN)
    ]
    mixing = jnp.concatenate([mix_ref[:, column] for column in columns], axis=1)
    for m in range(0, 8, 2):
        rows = [cot_refs[k][m * LANES : (m + 2) * LANES, :] for k in range(ZN)]
        part = lax.dot_general(
            mixing,
            jnp.concatenate(rows, axis=1),
            (((1,), (1,)), ((), ())),
            preferred_element_type=F32,
        )
        for n in range(2):
            at = (m + n) * (512 + GAP)
            scr[at : at + 512, :] = part[:, n * LANES : (n + 1) * LANES]
    for g in range(SEQ):
        for c in range(ZN):
            rows = [scr[pl.ds(c * LANES + i * SEQ + g, 8, stride=512 + GAP), :] for i in range(NCH)]
            out_ref[g * ZN + c] = jnp.concatenate(rows, axis=0).astype(BF16)


def grad_hidden_of(me, mixing, cot_parts):
    return pl.pallas_call(
        grad_hidden_kernel,
        out_shape=jax.ShapeDtypeStruct((SEQ * ZN, 32, LANES), BF16),
        in_specs=[sspec()] + [vspec()] * (1 + ZN),
        out_specs=vspec(),
        scratch_shapes=[VMEM((8 * (512 + GAP), LANES), F32)],
        compiler_params=params(),
        cost_estimate=cost(),
        name="grad_hidden",
    )(me, mixing, *cot_parts)


def forward_kernel(FWD, x_ref, rel_ref, t_ref, hid_ref, slope_ref, near, far):
    near[...] = jnp.zeros_like(near)
    far[...] = jnp.zeros_like(far)
    lane = lax.broadcasted_iota(jnp.int32, (8, LANES), 1)
    sub = lax.broadcasted_iota(jnp.int32, (8, LANES), 0)

    def before(now, old, by):
        return jnp.concatenate([old, now], axis=0)[old.shape[0] - by :][: now.shape[0]]

    def step(b, _):
        s = b * FWD
        rel = rel_ref[pl.ds(s, FWD)]
        inside = [rel >= 2**k for k in range(LEVELS)]
        for pair in range(0, NCH, 2):
            hidden = []
            for i in (pair, pair + 1):
                z = x_ref[pl.ds(s, FWD), i] * (t_ref[LEVELS * NCH + i] / SCALE)
                z = z.reshape(FWD, 4, 8, LANES)
                y = t_ref[16 * NCH + i] * z
                for k in range(LEVELS):
                    d = 2**k
                    if k < 8:
                        last = z[:, 3]
                        prev = before(last, near[k, i, pl.ds(3, 1)], 1)
                        near[k, i, pl.ds(3, 1)] = last[FWD - 1 :]
                        first = pltpu.roll(jnp.where(sub == 7, prev, last), 1, 1)
                        back = jnp.concatenate([first[:, None], z[:, :3]], axis=1)
                        if d < LANES:
                            back = pltpu.roll(jnp.where(lane >= LANES - d, back, z), d, 3)
                    elif k == 8:
                        last = z[:, 2:]
                        prev = before(last, near[k, i, pl.ds(2, 2)][None], 1)
                        near[k, i, pl.ds(2, 2)] = last[FWD - 1]
                        first = pltpu.roll(jnp.where(sub == 7, prev, last), 1, 2)
                        back = jnp.concatenate([first, z[:, :2]], axis=1)
                    elif k < 12:
                        by = 2 ** (k - 9)
                        prev = before(z, near[k, i][None], 1)
                        near[k, i] = z[FWD - 1]
                        back = pltpu.roll(jnp.where(sub >= 8 - by, prev, z), by, 2)
                    else:
                        by = 2 ** (k - 12)
                        old = far[k - 12, i]
                        back = before(z, old, by)
                        far[k - 12, i] = jnp.concatenate([old, z], axis=0)[FWD:]
                    z = z + t_ref[k * NCH + i] * jnp.where(inside[k], back, 0.0)
                    y = y + t_ref[(k + 17) * NCH + i] * z
                cdf = 0.5 * (1.0 + lax.erf(y * 0.7071067811865476))
                density = jnp.exp(-0.5 * y * y) * 0.3989422804014327
                slope_ref[i, pl.ds(s, FWD)] = cdf + y * density
                hidden.append(y * cdf)
            hid_ref[pl.ds(s, FWD), :, pl.ds(pair * 8, 16), :] = jnp.concatenate(
                hidden, axis=2
            ).astype(BF16)
        return 0

    lax.fori_loop(0, SEQ // FWD, step, 0)


def forward(x, rel, table):
    return pl.pallas_call(
        functools.partial(forward_kernel, FWD),
        out_shape=(
            jax.ShapeDtypeStruct((SEQ, ZN, 32, LANES), BF16),
            jax.ShapeDtypeStruct((NCH, SEQ, 4, 8, LANES), F32),
        ),
        in_specs=[vspec(), vspec(), sspec()],
        out_specs=(vspec(), vspec()),
        scratch_shapes=[
            VMEM((12, NCH, 4, 8, LANES), F32),
            VMEM((3, NCH, 4, 4, 8, LANES), F32),
        ],
        compiler_params=params(),
        cost_estimate=cost(),
        name="forward",
    )(x, rel, table)


def backward_kernel(BWD, gh_ref, slope_ref, rel_ref, t_ref, out_ref, near, far):
    near[...] = jnp.zeros_like(near)
    far[...] = jnp.zeros_like(far)
    lane = lax.broadcasted_iota(jnp.int32, (8, LANES), 1)
    sub = lax.broadcasted_iota(jnp.int32, (8, LANES), 0)

    def after(now, old, by):
        return jnp.concatenate([now, old], axis=0)[by:][: now.shape[0]]

    def step(b, _):
        s = SEQ - BWD - b * BWD
        rel = rel_ref[pl.ds(s, BWD)]
        inside = [rel >= 2**k for k in range(LEVELS)]
        for pair in range(0, NCH, 2):
            block = gh_ref[pl.ds(s, BWD), :, pl.ds(pair * 8, 16), :].astype(F32)
            for i in (pair, pair + 1):
                grad = block[:, :, (i - pair) * 8 : (i - pair + 1) * 8]
                grad = grad * slope_ref[i, pl.ds(s, BWD)]
                v = t_ref[31 * NCH + i] * grad
                for k in range(LEVELS - 1, -1, -1):
                    d = 2**k
                    p = jnp.where(inside[k], v, 0.0)
                    if k < 8:
                        head = p[:, 0]
                        foll = after(head, near[k, i, pl.ds(0, 1)], 1)
                        near[k, i, pl.ds(0, 1)] = head[:1]
                        end = pltpu.roll(jnp.where(sub == 0, foll, head), 7, 1)
                        ahead = jnp.concatenate([p[:, 1:], end[:, None]], axis=1)
                        if d < LANES:
                            ahead = pltpu.roll(jnp.where(lane < d, ahead, p), LANES - d, 3)
                    elif k == 8:
                        head = p[:, :2]
                        foll = after(head, near[k, i, pl.ds(0, 2)][None], 1)
                        near[k, i, pl.ds(0, 2)] = head[0]
                        end = pltpu.roll(jnp.where(sub == 0, foll, head), 7, 2)
                        ahead = jnp.concatenate([p[:, 2:], end], axis=1)
                    elif k < 12:
                        by = 2 ** (k - 9)
                        foll = after(p, near[k, i][None], 1)
                        near[k, i] = p[0]
                        ahead = pltpu.roll(jnp.where(sub < by, foll, p), 8 - by, 2)
                    else:
                        by = 2 ** (k - 12)
                        old = far[k - 12, i]
                        ahead = after(p, old, by)
                        far[k - 12, i] = jnp.concatenate([p, old], axis=0)[:4]
                    v = v + t_ref[(k + 16) * NCH + i] * grad + t_ref[k * NCH + i] * ahead
                out_ref[pl.ds(s, BWD), i] = v.reshape(BWD, 32, LANES).astype(BF16)
        return 0

    lax.fori_loop(0, SEQ // BWD, step, 0)


def backward(gh, slope, rel, table):
    return pl.pallas_call(
        functools.partial(backward_kernel, BWD),
        out_shape=jax.ShapeDtypeStruct((SEQ, NCH, LOCAL, LANES), BF16),
        in_specs=[vspec(), vspec(), vspec(), sspec()],
        out_specs=vspec(),
        scratch_shapes=[
            VMEM((12, NCH, 4, 8, LANES), F32),
            VMEM((3, NCH, 4, 4, 8, LANES), F32),
        ],
        compiler_params=params(),
        cost_estimate=cost(),
        name="backward",
    )(gh, slope, rel, table)


def hidden_tiles(hid_ref, scr):
    def load(j, _):
        scr[pl.ds(pl.multiple_of(j * (128 + GAP), 8), 128), :] = (
            hid_ref[pl.ds(j * 4, 4)].astype(F32).reshape(128, LANES)
        )
        return 0

    lax.fori_loop(0, SEQ, load, 0, unroll=4)
    for m in range(8):
        rows = [
            scr[pl.ds(c * 32 + i * 8 + m, SEQ, stride=LANES + GAP), :]
            for c in range(ZN)
            for i in range(NCH)
        ]
        yield m, slice(m * LANES, (m + 1) * LANES), jnp.concatenate(rows, axis=0)


def weigh_kernel(me_ref, hid_ref, held_ref, *refs):
    wg_refs, (scr, acc) = refs[:ZN], refs[ZN:]
    for m, at, h in hidden_tiles(hid_ref, scr):
        hb = h.astype(BF16)
        rows = jnp.concatenate([held_ref[k, at] for k in range(ZN)], axis=1)
        part = jnp.dot(hb, rows, preferred_element_type=F32)
        acc[...] = part if m == 0 else acc[...] + part
    for n in range(ZN):
        row = pl.multiple_of((me_ref[0] + n) % ZN * LANES, LANES)
        for k in range(ZN):
            column = pl.multiple_of((me_ref[0] + ZN - k) % ZN * LANES, LANES)
            t = acc[pl.ds(row, LANES), k * LANES : (k + 1) * LANES].T
            wg_refs[n][pl.ds(column, LANES), :] = t.astype(wg_refs[n].dtype)


def weigh(me, hid, held):
    return pl.pallas_call(
        weigh_kernel,
        out_shape=tuple(jax.ShapeDtypeStruct((512, LANES), BF16 if n else F32) for n in range(ZN)),
        in_specs=[sspec(), vspec(), vspec()],
        out_specs=(vspec(),) * ZN,
        scratch_shapes=[
            VMEM((SEQ * (LANES + GAP), LANES), F32),
            VMEM((512, 512), F32),
        ],
        compiler_params=params(),
        cost_estimate=cost(),
        name="weigh",
    )(me, hid, held)


def mix_kernel(me_ref, hid_ref, mix_ref, *refs):
    out_refs, scr = refs[:ZN], refs[ZN]
    columns = [
        pl.ds(pl.multiple_of((me_ref[0] + n) % ZN * LANES, LANES), LANES) for n in range(ZN)
    ]
    mixing = jnp.concatenate([mix_ref[:, column] for column in columns], axis=1)
    for m, at, h in hidden_tiles(hid_ref, scr):
        mixed = jnp.dot(h.T.astype(BF16), mixing, preferred_element_type=F32)
        for n in range(ZN):
            out_refs[n][at, :] = mixed[:, n * LANES : (n + 1) * LANES].astype(BF16)


def mix(me, hid, mixing):
    return pl.pallas_call(
        mix_kernel,
        out_shape=tuple(jax.ShapeDtypeStruct((ROWS, LANES), BF16) for _ in range(ZN)),
        in_specs=[sspec(), vspec(), vspec()],
        out_specs=(vspec(),) * ZN,
        scratch_shapes=[VMEM((SEQ * (LANES + GAP), LANES), F32)],
        compiler_params=params(),
        cost_estimate=cost(),
        name="mix",
    )(me, hid, mixing)


def total_kernel(in_ref, out_ref):
    out_ref[...] = jnp.sum(in_ref[...], axis=0)


def total(a):
    return pl.pallas_call(
        total_kernel,
        out_shape=jax.ShapeDtypeStruct(a.shape[1:], F32),
        in_specs=[vspec()],
        out_specs=vspec(),
        compiler_params=params(),
        cost_estimate=cost(),
        name="total",
    )(a)


def inner_kernel(v_ref, xt_ref, gain_ref, out_ref):
    sums = [jnp.zeros((LOCAL, LANES), F32) for _ in range(NCH)]
    for g in range(SEQ):
        for i in range(NCH):
            both = v_ref[g, i].astype(F32) * xt_ref[g, i].astype(F32)
            sums[i] = sums[i] + gain_ref[i * SEQ + g] * both
    out_ref[...] = (sums[0] + sums[1]) + (sums[2] + sums[3])


def inner(v, xt, gain):
    return pl.pallas_call(
        inner_kernel,
        out_shape=jax.ShapeDtypeStruct((LOCAL, LANES), F32),
        in_specs=[vspec(), vspec(), sspec()],
        out_specs=vspec(),
        compiler_params=params(),
        cost_estimate=cost(),
        name="inner",
    )(v, xt, gain)


def grad_in_kernel(v_ref, xt_ref, cot_ref, inv_ref, mean_ref, gain_ref, out_ref, scr):
    inv = inv_ref[...]
    scale = inv * inv * inv * mean_ref[...]

    for g in range(SEQ):
        for i in range(NCH):
            c = i * SEQ + g
            u = (gain_ref[c] * inv) * v_ref[g, i].astype(F32) - scale * xt_ref[g, i].astype(F32)
            scr[c * (LOCAL + GAP) : c * (LOCAL + GAP) + LOCAL, :] = u
    for m in range(LOCAL):
        at = slice(m * LANES, (m + 1) * LANES)
        u = scr[pl.ds(m % 4 * 8 + m // 4, LANES, stride=LOCAL + GAP), :].T
        out_ref[at, :] = (cot_ref[at, :].astype(F32) + u).astype(BF16)


def grad_in_of(v, xt, cot, inv, mean, gain):
    return pl.pallas_call(
        grad_in_kernel,
        out_shape=jax.ShapeDtypeStruct((LOCAL * LANES, LANES), BF16),
        in_specs=[vspec()] * 5 + [sspec()],
        out_specs=vspec(),
        scratch_shapes=[VMEM((LANES * (LOCAL + GAP), LANES), F32)],
        compiler_params=params(),
        cost_estimate=cost(),
        name="grad_in",
    )(v, xt, cot, inv, mean, gain)


def exchange(a, axes):
    return lax.all_to_all(a, axes, 0, 0, tiled=True)


def sum_over_ch(a):
    total = a
    for by in (1, 2, 3):
        total = total + turned(a, by)
    return total


def turned(a, by):
    return lax.ppermute(a, "ch", [(j, (j + by) % ZN) for j in range(ZN)]) if by else a


def parts_of(a, me):
    a = a.reshape(8, ZN, LANES, LANES)
    return [
        turned(
            lax.dynamic_index_in_dim(a, (me + k) % ZN, 1, False).reshape(ROWS, LANES), k
        )
        for k in range(ZN)
    ]


def whole_kernel(me_ref, x_ref, *refs):
    parts, out_ref = refs[:ZN], refs[ZN]
    for k in range(ZN):
        r = (me_ref[0] + ZN - k) % ZN
        for n in range(8):
            part = parts[k][n * LANES : (n + 1) * LANES, :].astype(F32)
            out_ref[n, r] = (x_ref[n, r].astype(F32) + part).astype(BF16)


def whole_of(x, parts, place):
    shape = (8, ZN, LANES, LANES)
    return pl.pallas_call(
        whole_kernel,
        out_shape=jax.ShapeDtypeStruct(shape, BF16),
        in_specs=[sspec()] + [vspec()] * (1 + ZN),
        out_specs=vspec(),
        compiler_params=params(),
        cost_estimate=cost(),
        name="whole",
    )(place, x.reshape(shape), *parts).reshape(LOCAL * LANES, LANES)


def after(later, first):
    return lax.optimization_barrier((later, first))[0]


def per_device(tokens, norm_gain, low_taps, high_taps, level_gain, mixing, lengths, cotangent):
    both = ("seq", "ch")
    g = lax.axis_index("seq")
    full = mixing.shape[0]
    bases = LOCAL * LANES * SEQ

    me = lax.axis_index("ch")
    place = me.reshape(1)

    x = tokens.astype(F32)
    squares = jnp.sum(x * x, axis=1).reshape(8, ZN, LANES).swapaxes(0, 1).reshape(LOCAL, LANES)
    inv = lax.rsqrt(sum_over_ch(squares) / full + EPS)
    cot_parts = parts_of(after(cotangent, squares), me)
    xt = turn(tokens)
    x_sent = (xt.astype(F32) * (inv * SCALE)).astype(jnp.float16)
    x_sent = exchange(x_sent, "seq")
    x_seq = x_sent.astype(F32)
    rel, table = prepare(lengths, low_taps, high_taps, level_gain, norm_gain)
    table = lax.dynamic_index_in_dim(table.reshape(32, NCH, SEQ), g, 2, False).reshape(-1)
    gh = grad_hidden_of(after(place, table), mixing, cot_parts)
    gh_seq = exchange(after(gh, x_sent), both).reshape(SEQ, ZN, 32, LANES)
    held = jnp.stack(cot_parts)
    hid, slope = forward(x_seq, rel, table)
    hid_rows = exchange(after(hid, gh_seq).reshape(SEQ * ZN, 32, LANES), both)
    v = exchange(after(backward(gh_seq, after(slope, held), rel, table), hid_rows), "seq")
    shares = weigh(place, hid_rows, held)
    own_first = shares[0]
    shares = [turned(shares[n], n).astype(F32) for n in range(ZN)]
    wg = (shares[0] + shares[1] + shares[2] + shares[3]) / math.sqrt(bases)
    mixed = mix(after(place, own_first), hid_rows, mixing)
    parts = [turned(mixed[n], n) for n in range(ZN)]
    own = inner(v, xt, norm_gain)
    wg = exchange(after(wg, own).reshape(SEQ, 16, LANES), "seq")
    others = [turned(own, k) for k in range(1, ZN)]
    mean = (own + others[0] + others[1] + others[2]) / full
    grad_in = grad_in_of(v, xt, cotangent, inv, mean, norm_gain)
    weight_grad = total(after(wg, grad_in)).T
    layer_out = whole_of(tokens, parts, place)
    return (layer_out, grad_in, weight_grad)


def solution(mesh):
    in_specs = (
        P("seq", "ch"),
        P("ch"),
        P(None, None, "ch"),
        P(None, None, "ch"),
        P(None, "ch"),
        P(),
        P(),
        P("seq", "ch"),
    )
    out_specs = (P("seq", "ch"), P("seq", "ch"), P("ch", "seq"))
    return jax.shard_map(
        per_device, mesh=mesh, in_specs=in_specs, out_specs=out_specs, check_vma=False
    )
```
